128 devices in a mesh: gx: 8 (over y, core), gy: 16 (over z, x).
Axes of the slice: x: 4, y: 4, z: 4, core: 2. Of those that a mesh axis runs over, the one named last changes fastest.
Arguments:
- pixels: int32 [32, 32, 4, 131072], P('gy', 'gx'), may hold values from 0 to 255, as said below
- weights: bfloat16 [32, 32, 4, 131072], P('gy', 'gx'), may hold values from 0.25 to 1
- adjacency: int32 [2, 32, 32], replicated, may hold values 0 or 1
Outputs:
- log_gain: float32 [32, 32], P('gy', 'gx')
The draws below stay inside these ranges and needn't reach their ends.
Inputs may be any that keep to these rules, and one draw needn't show every extreme that they name: `pixels`: bin indices of 8-bit intensities. `adjacency`: entry [0, r, c] is 1 where tile (r, c) and the tile to its right share a usable border, entry [1, r, c] likewise for the tile below; entries of pairs beyond the grid's edge are read by no output.
All inputs are finite; a program needn't handle non-finite values.
Results may differ from the reference program's by a relative error of at most 0.0003.
Values may be sent and summed in bfloat16 or wider, within the bound.
No kernel may reach another device: no remote copies, remote signals or barrier semaphores. Data moves between devices by JAX's collectives and lax.ppermute only.
A program may use at most 128 MiB of HBM per device.

```python
import math
import jax
import jax.numpy as jnp
from jax import lax

SEG = 1024
STRIP = 128
ITERS = 20
GR = 32
GC = 32


def draw_pixels(key, part):
    offset_key = jax.random.fold_in(key, 11)
    spread_key = jax.random.fold_in(key, 12)
    jitter_key = jax.random.fold_in(key, 13)
    slope_key = jax.random.fold_in(key, 14)
    length = STRIP * SEG
    column = jnp.arange(GC, dtype=jnp.int32)
    drift = 32 * column // GC
    baseline = drift[None, :] + jax.random.randint(offset_key, (GR, GC), 0, 32, dtype=jnp.int32)
    slope = jax.random.randint(slope_key, (GR, GC, 4, 1), -80, 81, dtype=jnp.int32)
    position = jnp.arange(length, dtype=jnp.int32)[None, None, None, :]
    ramp = 80 + slope * position // length
    spread = jax.random.randint(spread_key, (GR, GC, 4), 20, 61, dtype=jnp.int32)
    jitter = jax.random.randint(jitter_key, (GR, GC, 4, length), 0, spread[..., None], dtype=jnp.int32)
    return jnp.clip(baseline[:, :, None, None] + ramp + jitter, 0, 255).astype(jnp.int32)


def draw_weights(key, part):
    phase_key = jax.random.fold_in(key, 21)
    rough_key = jax.random.fold_in(key, 22)
    length = STRIP * SEG
    along = jnp.arange(length, dtype=jnp.float32) / length
    phase = jax.random.uniform(phase_key, (GR, GC, 4, 1), jnp.float32, -math.pi, math.pi)
    wave = 0.5 + 0.5 * jnp.sin(math.pi * along[None, None, None, :] + phase)
    rough = jax.random.uniform(rough_key, (GR, GC, 4, length), jnp.float32, 0.7, 1.0)
    profile = wave
    return (0.25 + 0.75 * rough * profile).astype(jnp.bfloat16)


def set_ends(array, key, smallest, top_value):
    spot = [jax.random.randint(jax.random.fold_in(key, axis), (), 0, length) for axis, length in enumerate(array.shape)]
    widest = array.shape.index(max(array.shape))
    neighbour = spot[:widest] + [(spot[widest] + 1) % array.shape[widest]] + spot[widest + 1:]
    return array.at[tuple(spot)].set(smallest).at[tuple(neighbour)].set(top_value)


def setup_inputs(seed: int = 0) -> dict:
    arg_keys = jax.random.split(jax.random.key(seed), 4)
    pixels = draw_pixels(jax.random.fold_in(arg_keys[3], 71), 0)
    weights = draw_weights(jax.random.fold_in(arg_keys[3], 71), 0)
    adjacency = set_ends((jax.random.randint(arg_keys[2], (2, GR, GC), 0, 8) < 7).astype(jnp.int32), jax.random.fold_in(arg_keys[2], 1), 0, 1)
    return dict(pixels=pixels, weights=weights, adjacency=adjacency)


anchor_weight = 0.5
mismatch_scale = 8.0


def strip_stats(strip_hist):
    totals = jnp.sum(strip_hist, axis=-1)
    centres = jnp.arange(256, dtype=jnp.float32) + 0.5
    means = jnp.sum(strip_hist * centres, axis=-1) / totals
    cumulative = jnp.cumsum(strip_hist, axis=-1) / totals[..., None]
    return means, cumulative


def pair_terms(own_hist, other_hist, usable):
    own_mean, own_cdf = strip_stats(own_hist)
    other_mean, other_cdf = strip_stats(other_hist)
    distance = jnp.sum(jnp.abs(own_cdf - other_cdf), axis=-1)
    mismatch = (distance - jnp.abs(own_mean - other_mean)) / mismatch_scale
    present = usable > 0
    confidence = jnp.where(present, 1.0 / (0.25 + mismatch * mismatch), 0.0)
    offsets = jnp.where(present, jnp.log(other_mean) - jnp.log(own_mean), 0.0)
    return confidence, offsets


def relax_step(padded, confidence, offsets):
    beside = jnp.stack([padded[:-2, 1:-1], padded[2:, 1:-1], padded[1:-1, :-2], padded[1:-1, 2:]], axis=-1)
    return jnp.sum(confidence * (beside + offsets), axis=-1)


def reference(pixels, weights, adjacency):
    length = pixels.shape[3]

    def row_histogram(row_index):
        own_pixels = lax.dynamic_index_in_dim(pixels, row_index, 0, False)
        own_weights = lax.dynamic_index_in_dim(weights, row_index, 0, False).astype(jnp.float32)
        below_index = jnp.minimum(row_index + 1, GR - 1).astype(jnp.int32)
        above_index = jnp.maximum(row_index - 1, 0).astype(jnp.int32)
        from_below = lax.dynamic_index_in_dim(weights, below_index, 0, False)[:, 0].astype(jnp.float32)
        from_below = from_below * (row_index + 1 < GR).astype(jnp.float32)
        from_above = lax.dynamic_index_in_dim(weights, above_index, 0, False)[:, 1].astype(jnp.float32)
        from_above = from_above * (row_index > 0).astype(jnp.float32)
        zero_strip = jnp.zeros((1, length), jnp.float32)
        from_left = jnp.concatenate([zero_strip, own_weights[:-1, 3]], axis=0)
        from_right = jnp.concatenate([own_weights[1:, 2], zero_strip], axis=0)
        partner = jnp.stack([from_above, from_below, from_left, from_right], axis=1)
        joint_weight = lax.optimization_barrier((own_weights * partner).astype(jnp.bfloat16)).astype(jnp.float32)
        strip_ids = (jnp.arange(GC * 4, dtype=jnp.int32) * 256)[:, None]
        segment = (strip_ids + own_pixels.reshape(GC * 4, length).astype(jnp.int32)).reshape(-1)
        bin_sums = jax.ops.segment_sum(joint_weight.reshape(-1), segment, num_segments=GC * 4 * 256)
        return bin_sums.reshape(GC, 4, 256)

    strip_hist = lax.map(row_histogram, jnp.arange(GR, dtype=jnp.int32))
    zero_row = jnp.zeros((1, GC, 256), jnp.float32)
    zero_column = jnp.zeros((GR, 1, 256), jnp.float32)
    from_above = jnp.concatenate([zero_row, strip_hist[:-1, :, 1]], axis=0)
    from_below = jnp.concatenate([strip_hist[1:, :, 0], zero_row], axis=0)
    from_left = jnp.concatenate([zero_column, strip_hist[:, :-1, 3]], axis=1)
    from_right = jnp.concatenate([strip_hist[:, 1:, 2], zero_column], axis=1)
    partner_hist = jnp.stack([from_above, from_below, from_left, from_right], axis=2)
    across = adjacency[0].astype(jnp.int32)
    downward = adjacency[1].astype(jnp.int32)
    zero_links_row = jnp.zeros((1, GC), jnp.int32)
    zero_links_column = jnp.zeros((GR, 1), jnp.int32)
    up_valid = jnp.concatenate([zero_links_row, downward[:-1]], axis=0)
    down_valid = jnp.concatenate([downward[:-1], zero_links_row], axis=0)
    left_valid = jnp.concatenate([zero_links_column, across[:, :-1]], axis=1)
    right_valid = jnp.concatenate([across[:, :-1], zero_links_column], axis=1)
    usable = jnp.stack([up_valid, down_valid, left_valid, right_valid], axis=-1)
    confidence, offsets = pair_terms(strip_hist, partner_hist, usable)
    denominator = anchor_weight + jnp.sum(confidence, axis=-1)
    log_gain = jnp.zeros((GR, GC), jnp.float32)
    for sweep_index in range(ITERS):
        updated = relax_step(jnp.pad(log_gain, 1), confidence, offsets) / denominator
        log_gain = updated - jnp.sum(updated) / (GR * GC)
    return log_gain
```

```python
import functools

import jax
import jax.numpy as jnp
import numpy as np
from jax import lax
from jax.experimental import pallas as pl
from jax.experimental.pallas import tpu as pltpu
from jax.sharding import PartitionSpec as P

ITERS = 20
ROWS, COLS = 2, 4
CHUNKS, LANES = 1024, 128
LINES = 4 * CHUNKS
GROUP = 16
ALL = ("gx", "gy")
F32, BF16, I32 = jnp.float32, jnp.bfloat16, jnp.int32
VMEM_BYTES = 56 << 20

anchor_weight = 0.5
mismatch_scale = 8.0

INNER = np.array(
    [(c, 1, 4 + c, 0) for c in range(4)]
    + [(4 * r + c, 3, 4 * r + c + 1, 2) for r in range(2) for c in range(3)],
    np.int32,
)
OUTER = np.array([(4, 1), (5, 1), (2, 0), (3, 0), (0, 2), (4, 2)], np.int32)


def by_lines(array):
    tiles = array.reshape(ROWS * COLS, 4, CHUNKS, LANES)
    return tiles.transpose(0, 2, 1, 3).reshape(ROWS * COLS, LINES, LANES)


def pack_kernel(side, lines, px_ref, w_ref, out_ref, wide):
    count = lines // 4
    out_ref[0, 0] = px_ref[0, pl.ds(side, count, stride=4), :].astype(F32).astype(BF16)
    wide[...] = w_ref[0].astype(F32)
    out_ref[0, 1] = wide[pl.ds(side, count, stride=4), :].astype(BF16)


def packed(px, w, first, step, side):
    lines = 1024
    return pl.pallas_call(
        functools.partial(pack_kernel, side, lines),
        grid=(2, LINES // lines),
        in_specs=[
            pl.BlockSpec((1, lines, LANES), lambda n, k: (first + step * n, k, 0)),
            pl.BlockSpec((1, lines, LANES), lambda n, k: (first + step * n, k, 0)),
        ],
        out_specs=pl.BlockSpec((1, 2, lines // 4, LANES), lambda n, k: (n, 0, k, 0)),
        out_shape=jax.ShapeDtypeStruct((2, 2, CHUNKS, LANES), BF16),
        scratch_shapes=[pltpu.VMEM((lines, LANES), F32)],
        compiler_params=pltpu.CompilerParams(vmem_limit_bytes=VMEM_BYTES),
        cost_estimate=pl.CostEstimate(flops=1 << 20, bytes_accessed=7 << 20, transcendentals=0),
    )(px, w)


def one_hot_pair(bins, joint):
    upper = lax.shift_right_logical(bins, 4).astype(F32).astype(BF16)
    lower = (bins & 15).astype(F32).astype(BF16)
    zero, one = jnp.zeros((), BF16), jnp.ones((), BF16)
    left = [jnp.where(upper == BF16(k), joint, zero) for k in range(16)]
    right = [jnp.where(lower == BF16(k), one, zero) for k in range(16)]
    return jnp.concatenate(left, 0), jnp.concatenate(right, 0)


def diagonal_sum(left, right):
    product = lax.dot_general(
        jnp.concatenate(left, 1),
        jnp.concatenate(right, 1),
        (((1,), (1,)), ((), ())),
        preferred_element_type=F32,
    )
    column = lax.broadcasted_iota(I32, (GROUP, 256), 1) % GROUP
    row = lax.broadcasted_iota(I32, (GROUP, 256), 0)
    kept = jnp.where((column == row)[None], product.reshape(16, GROUP, 256), 0.0)
    return jnp.sum(kept, axis=1)


def inner_kernel(table, px_a, px_b, w_a, w_b, out_ref, wide_a, wide_b):
    n = pl.program_id(0)
    side_a, side_b = table[n, 1], table[n, 3]
    ops_a, ops_b = [], []
    for v in range(CHUNKS // GROUP):
        o = 4 * GROUP * v
        wide_a[o : o + 64] = w_a[0, o : o + 64].astype(F32)
        wide_b[o : o + 64] = w_b[0, o : o + 64].astype(F32)
        rows_a = pl.ds(o + side_a, GROUP, stride=4)
        rows_b = pl.ds(o + side_b, GROUP, stride=4)
        joint = (wide_a[rows_a, :] * wide_b[rows_b, :]).astype(BF16)
        ops_a.append(one_hot_pair(px_a[0, rows_a, :], joint))
        ops_b.append(one_hot_pair(px_b[0, rows_b, :], joint))
    for place, ops in enumerate((ops_a, ops_b)):
        out_ref[0, place] = diagonal_sum(*zip(*ops))


def inner_sums(px, w):
    count = len(INNER)
    tile = lambda which: pl.BlockSpec((1, LINES, LANES), lambda n, t: (t[n, which], 0, 0))
    return pl.pallas_call(
        inner_kernel,
        grid_spec=pltpu.PrefetchScalarGridSpec(
            num_scalar_prefetch=1,
            grid=(count,),
            in_specs=[tile(0), tile(2), tile(0), tile(2)],
            out_specs=pl.BlockSpec((1, 2, 16, 256), lambda n, t: (n, 0, 0, 0)),
            scratch_shapes=[pltpu.VMEM((LINES, LANES), F32)] * 2,
        ),
        out_shape=jax.ShapeDtypeStruct((count, 2, 16, 256), F32),
        compiler_params=pltpu.CompilerParams(vmem_limit_bytes=VMEM_BYTES),
        cost_estimate=pl.CostEstimate(
            flops=count * 2 * 2 * 256 * 256 * 8192, bytes_accessed=count * (6 << 20), transcendentals=0
        ),
    )(jnp.asarray(INNER), px, px, w, w)


def f32_dot(a, b):
    return jnp.dot(a, b, precision=lax.Precision.HIGHEST, preferred_element_type=F32)


def pair_results(first, second):
    lower = lax.broadcasted_iota(I32, (256, 384), 0) // GROUP
    column = lax.broadcasted_iota(I32, (256, 384), 1)
    within = ((column < 16) & (lower <= column)) | ((column >= 128) & (column < 256))
    maps = jnp.where(column >= 256, lower.astype(F32) + 0.5, within.astype(F32))
    by_first, by_second = f32_dot(first, maps), f32_dot(second, maps)
    row = lax.broadcasted_iota(I32, (256, 256), 0)
    other = lax.broadcasted_iota(I32, (256, 256), 1)
    same_pair = row // 16 == other // 16
    all_of_pair = same_pair.astype(F32)
    before = (same_pair & (other < row)).astype(F32)
    base = (lax.broadcasted_iota(I32, (256, 128), 0) % 16 * 16).astype(F32)
    total_first = by_first[:, 128:256]
    difference = by_first - by_second
    cumulative = difference[:, :128] + f32_dot(before, difference[:, 128:256])
    moment_first = by_first[:, 256:] + base * total_first
    moment_second = by_second[:, 256:] + base * by_second[:, 128:256]
    lane = lax.broadcasted_iota(I32, (256, 128), 1)
    parts = jnp.concatenate(
        [total_first, moment_first, moment_second, jnp.where(lane < 16, jnp.abs(cumulative), 0.0)], 1
    )
    sums = f32_dot(all_of_pair, parts)
    total = sums[:, :128]
    mean_first, mean_second = sums[:, 128:256] / total, sums[:, 256:384] / total
    distance = jnp.sum(sums[:, 384:], axis=1, keepdims=True) / total
    mismatch = (distance - jnp.abs(mean_first - mean_second)) / mismatch_scale
    confidence = 1.0 / (0.25 + mismatch * mismatch)
    offset = jnp.log(mean_second) - jnp.log(mean_first)
    mine = lax.broadcasted_iota(I32, (256, 128), 0)
    spread = jnp.where(mine == 16 * lane, confidence, jnp.where(mine == 16 * (lane - 16), offset, 0.0))
    spread = jnp.where(total > 0, spread, 0.0)
    return jnp.sum(spread, axis=0, keepdims=True)


def outer_kernel(table, px_ref, w_ref, below, above, left, inner, out_ref, wide, firsts, seconds):
    n = pl.program_id(0)
    side = table[n, 1]
    ops_own, ops_far = [], []
    for v in range(CHUNKS // GROUP):
        o = 4 * GROUP * v
        wide[o : o + 64] = w_ref[0, o : o + 64].astype(F32)
        rows = pl.ds(o + side, GROUP, stride=4)
        dense = slice(GROUP * v, GROUP * (v + 1))

        def far(k):
            return jnp.where(
                n < 2, below[0, k, dense], jnp.where(n < 4, above[0, k, dense], left[0, k, dense])
            )

        joint = (wide[rows, :] * far(1).astype(F32)).astype(BF16)
        ops_own.append(one_hot_pair(px_ref[0, rows, :], joint))
        ops_far.append(one_hot_pair(far(0).astype(F32).astype(I32), joint))
    own, other = diagonal_sum(*zip(*ops_own)), diagonal_sum(*zip(*ops_far))
    done = len(INNER)
    place = pl.ds(pl.multiple_of((done + n) * 16, 16), 16)
    firsts[place, :] = jnp.where(n < 2, own, other)
    seconds[place, :] = jnp.where(n < 2, other, own)

    @pl.when(n == len(OUTER) - 1)
    def _():
        firsts[: done * 16] = inner[:, 0].reshape(done * 16, 256)
        seconds[: done * 16] = inner[:, 1].reshape(done * 16, 256)
        out_ref[...] = jnp.broadcast_to(pair_results(firsts[...], seconds[...]), out_ref.shape)


def outer_results(px, w, below, above, left, inner, devices):
    count = len(OUTER)
    tile = pl.BlockSpec((1, LINES, LANES), lambda n, t: (t[n, 0], 0, 0))
    strip = lambda low: pl.BlockSpec(
        (1, 2, CHUNKS, LANES), lambda n, t: (jnp.clip(n - low, 0, 1), 0, 0, 0)
    )
    return pl.pallas_call(
        outer_kernel,
        grid_spec=pltpu.PrefetchScalarGridSpec(
            num_scalar_prefetch=1,
            grid=(count,),
            in_specs=[
                tile, tile, strip(0), strip(2), strip(4),
                pl.BlockSpec(inner.shape, lambda n, t: (0, 0, 0, 0)),
            ],
            out_specs=pl.BlockSpec((devices, LANES), lambda n, t: (0, 0)),
            scratch_shapes=[
                pltpu.VMEM((LINES, LANES), F32),
                pltpu.VMEM((256, 256), F32),
                pltpu.VMEM((256, 256), F32),
            ],
        ),
        out_shape=jax.ShapeDtypeStruct((devices, LANES), F32),
        compiler_params=pltpu.CompilerParams(vmem_limit_bytes=VMEM_BYTES),
        cost_estimate=pl.CostEstimate(
            flops=count * 2 * 2 * 256 * 256 * 8192, bytes_accessed=count * (4 << 20), transcendentals=0
        ),
    )(jnp.asarray(OUTER), px, w, below, above, left, inner)


def on_grid(gathered, height, count_y):
    devices = gathered.shape[0]
    slot = lax.broadcasted_iota(I32, (LANES, LANES), 0)
    lane = lax.broadcasted_iota(I32, (LANES, LANES), 1)
    c, odd, right = lane % 4, lane // 32 % 2, lane // 64 == 1
    offset_slots = 16 * odd
    edge = right & (c == 3)
    slots = [
        jnp.where(edge, 14, jnp.where(right, 4 + c, c)),
        jnp.where(edge, 15, jnp.where(right, 7 + c, jnp.where(c < 2, 10 + c, -100))),
        jnp.where(right | (c < 2), -100, 10 + c),
    ]
    choose = jnp.concatenate([(slot == s + offset_slots).astype(F32) for s in slots], 1)
    chosen = f32_dot(gathered, choose)
    device = lax.broadcasted_iota(I32, (devices, LANES), 0)
    lane = lax.broadcasted_iota(I32, (devices, LANES), 1)
    shifted = ((lane // 64 == 1) & (lane % 4 == 3)).astype(I32)
    here = device // count_y == lane % 32 // 4 + shifted
    parts = [jnp.where(here, chosen[:, LANES * k : LANES * (k + 1)], 0.0) for k in range(3)]
    row = lax.broadcasted_iota(I32, (height, devices), 0)
    top = lax.broadcasted_iota(I32, (height, devices), 1) % count_y * 2
    place = jnp.concatenate([(row == top + k).astype(F32) for k in (0, 1, -1)], 1)
    return f32_dot(place, jnp.concatenate(parts, 0))


def sweep_kernel(height, width, count_y, where_ref, gathered, adjacency, out_ref, links, gain_ref):
    grid = on_grid(gathered[...], height, count_y)
    links[...] = jnp.zeros_like(links)
    links[:, :, :width] = adjacency[...]
    row = lax.broadcasted_iota(I32, (height, LANES), 0)
    column = lax.broadcasted_iota(I32, (height, LANES), 1)
    below = (links[1] > 0) & (row < height - 1) & (column < width)
    beside = (links[0] > 0) & (column < width - 1)

    def lanes_of(k, present):
        values = grid if k == 0 else pltpu.roll(grid, LANES - 32 * k, 1)
        return jnp.where(present, values, 0.0)

    conf_down, off_down = lanes_of(0, below), lanes_of(1, below)
    conf_right, off_right = lanes_of(2, beside), lanes_of(3, beside)
    up = lambda a: pltpu.roll(a, 1, 0)
    down = lambda a: pltpu.roll(a, height - 1, 0)
    lefts = lambda a: pltpu.roll(a, 1, 1)
    rights = lambda a: pltpu.roll(a, LANES - 1, 1)
    conf_up, off_up = up(conf_down), -up(off_down)
    conf_left, off_left = lefts(conf_right), -lefts(off_right)
    scale = 1.0 / (anchor_weight + conf_up + conf_down + conf_left + conf_right)
    constant = scale * (
        conf_up * off_up + conf_down * off_down + conf_left * off_left + conf_right * off_right
    )
    a_up, a_down, a_left, a_right = (scale * a for a in (conf_up, conf_down, conf_left, conf_right))

    def sweep(_, gain):
        fresh = (
            (a_up * up(gain) + a_down * down(gain))
            + (a_left * lefts(gain) + a_right * rights(gain))
            + constant
        )
        return fresh - jnp.sum(fresh) / (height * width)

    gain = lax.fori_loop(0, ITERS, sweep, jnp.zeros((height, LANES), F32), unroll=True)
    gain_ref[...] = pltpu.roll(gain, LANES - where_ref[1] * COLS, 1)
    out_ref[...] = gain_ref[pl.ds(where_ref[0] * ROWS, ROWS), :COLS]


def sweeps(gathered, adjacency, where):
    height, width = adjacency.shape[1:]
    return pl.pallas_call(
        functools.partial(sweep_kernel, height, width, height // ROWS),
        in_specs=[
            pl.BlockSpec(memory_space=pltpu.SMEM),
            pl.BlockSpec(memory_space=pltpu.VMEM),
            pl.BlockSpec(memory_space=pltpu.VMEM),
        ],
        out_specs=pl.BlockSpec(memory_space=pltpu.VMEM),
        out_shape=jax.ShapeDtypeStruct((ROWS, COLS), F32),
        scratch_shapes=[pltpu.VMEM((2, height, LANES), I32), pltpu.VMEM((height, LANES), F32)],
    )(where, gathered, adjacency)


def body(pixels, weights, adjacency):
    px, w = by_lines(pixels), by_lines(weights)
    count_x, count_y = lax.axis_size("gx"), lax.axis_size("gy")
    ahead = lambda n: [(i, i + 1) for i in range(n - 1)]
    back = lambda n: [(i + 1, i) for i in range(n - 1)]
    below = lax.ppermute(packed(px, w, 0, 1, 0), "gy", back(count_y))
    above = lax.ppermute(packed(px, w, 6, 1, 1), "gy", ahead(count_y))
    left = lax.ppermute(packed(px, w, 3, 4, 3), "gx", ahead(count_x))
    inner = inner_sums(px, w)
    results = outer_results(px, w, below, above, left, inner, count_x * count_y)
    gathered = lax.all_to_all(results, ALL, 0, 0, tiled=True)
    where = jnp.stack([lax.axis_index("gy"), lax.axis_index("gx")]).astype(I32)
    return sweeps(gathered, adjacency, where)


def solution(mesh):
    return jax.shard_map(
        body,
        mesh=mesh,
        in_specs=(P("gy", "gx", None, None), P("gy", "gx", None, None), P()),
        out_specs=P("gy", "gx"),
        check_vma=False,
    )
```

```python
import functools

import jax
import jax.numpy as jnp
import numpy as np
from jax import lax
from jax.experimental import pallas as pl
from jax.experimental.pallas import tpu as pltpu
from jax.sharding import PartitionSpec as P

ITERS = 20
ROWS, COLS = 2, 4
CHUNKS, LANES = 1024, 128
LINES = 4 * CHUNKS
BATCH = 2
GROUP = 16
ALL = ("gx", "gy")
F32, BF16, I32 = jnp.float32, jnp.bfloat16, jnp.int32
VMEM_BYTES = 48 << 20

anchor_weight = 0.5
mismatch_scale = 8.0

INNER = np.array(
    [(c, 1, 4 + c, 0) for c in range(4)]
    + [(4 * r + c, 3, 4 * r + c + 1, 2) for r in range(2) for c in range(3)],
    np.int32,
)
SENT = (((0, 0), (1, 0)), ((6, 1), (7, 1)), ((3, 3), (7, 3)))
OUTER = np.array([(4, 1), (5, 1), (2, 0), (3, 0), (0, 2), (4, 2)], np.int32)


def pack_kernel(px, w, below_ref, above_ref, left_ref, pixels, tiles, wide, px_arrived, w_arrived):
    jobs = [(out, n) + SENT[k][n] for k, out in enumerate((below_ref, above_ref, left_ref)) for n in range(2)]
    needed = sorted({job[2] for job in jobs}, key=[job[2] for job in jobs].index)
    w_copies = [
        pltpu.make_async_copy(w.at[tile], tiles.at[k], w_arrived.at[k]) for k, tile in enumerate(needed)
    ]
    px_copies = [
        pltpu.make_async_copy(px.at[job[2], :, job[3], :], pixels.at[k], px_arrived.at[k])
        for k, job in enumerate(jobs)
    ]
    for copy in w_copies + px_copies:
        copy.start()
    for k, tile in enumerate(needed):
        w_copies[k].wait()
        wide[k % 2] = tiles[k].astype(F32)
        for out, n, _, side in (job for job in jobs if job[2] == tile):
            out[n, 1] = wide[k % 2, pl.ds(side, CHUNKS, stride=4), :].astype(BF16)
    for k, (out, n, _, _) in enumerate(jobs):
        px_copies[k].wait()
        out[n, 0] = pixels[k].astype(F32).astype(BF16)


def packed(px, w):
    strips = jax.ShapeDtypeStruct((2, 2, CHUNKS, LANES), BF16)
    vmem = pl.BlockSpec(memory_space=pltpu.VMEM)
    return pl.pallas_call(
        pack_kernel,
        in_specs=[pl.BlockSpec(memory_space=pl.ANY)] * 2,
        out_specs=[vmem] * 3,
        out_shape=[strips] * 3,
        scratch_shapes=[
            pltpu.VMEM((6, CHUNKS, LANES), I32),
            pltpu.VMEM((5, LINES, LANES), BF16),
            pltpu.VMEM((2, LINES, LANES), F32),
            pltpu.SemaphoreType.DMA((6,)),
            pltpu.SemaphoreType.DMA((5,)),
        ],
        compiler_params=pltpu.CompilerParams(vmem_limit_bytes=VMEM_BYTES),
        cost_estimate=pl.CostEstimate(flops=1 << 20, bytes_accessed=8 << 20, transcendentals=0),
    )(px, w)


def one_hot_pair(bins, joint):
    upper = lax.shift_right_logical(bins, 4).astype(F32).astype(BF16)
    lower = (bins & 15).astype(F32).astype(BF16)
    zero, one = jnp.zeros((), BF16), jnp.ones((), BF16)
    left = [jnp.where(upper == BF16(k), joint, zero) for k in range(16)]
    right = [jnp.where(lower == BF16(k), one, zero) for k in range(16)]
    return jnp.concatenate(left, 0), jnp.concatenate(right, 0)


def diagonal_sum(product):
    column = lax.broadcasted_iota(I32, (GROUP, 256), 1) % GROUP
    row = lax.broadcasted_iota(I32, (GROUP, 256), 0)
    kept = jnp.where((column == row)[None], product.reshape(16, GROUP, 256), 0.0)
    return jnp.sum(kept, axis=1)


def strip_products(sums, strips):
    for part in range(CHUNKS // GROUP // 2):
        pairs = zip(*(strips(2 * part + half) for half in range(2)))
        for unit, halves in enumerate(pairs):
            left, right = zip(*(one_hot_pair(bins, joint) for bins, joint in halves))
            pltpu.matmul_push_rhs(jnp.concatenate(right, 1), part % 2, unit, transpose=True)
            pltpu.matmul_acc_lhs(sums[unit], jnp.concatenate(left, 1), load_staged_rhs=part % 2)


def with_sums(function):
    units = [pltpu.ACC(unit)((256, 256), F32) for _ in range(BATCH) for unit in range(2)]
    pl.run_scoped(lambda *refs: function([refs[:2], refs[2:]]), *units)


def entry(table, step, column):
    values = [int(v) for v in table[:, column]]
    chosen = jnp.int32(values[0])
    for k in range(1, len(values)):
        if values[k] != values[k - 1]:
            chosen = jnp.where(step >= k, jnp.int32(values[k]), chosen)
    return chosen


def fetch(px, w, table, step, buffers, tiles, arrived, slot, item):
    tile, side = entry(table, step, 2 * item), entry(table, step, 2 * item + 1)
    return (
        pltpu.make_async_copy(px.at[tile, :, side, :], buffers.at[slot, item], arrived.at[slot, item, 0]),
        pltpu.make_async_copy(w.at[tile], tiles.at[slot, item], arrived.at[slot, item, 1]),
    )


def start_next(items, *refs):
    n, steps = pl.program_id(0), pl.num_programs(0)
    px, w, table, buffers, tiles, arrived = refs
    slot = lax.rem(n, 2)

    def start(step, place):
        for item in range(items):
            for copy in fetch(px, w, table, step, buffers, tiles, arrived, place, item):
                copy.start()

    @pl.when(n == 0)
    def _():
        start(0, 0)

    @pl.when(n + 1 < steps)
    def _():
        start(n + 1, 1 - slot)

    return slot


def side_of(tiles, wide, slot, item, side, v):
    o = 4 * GROUP * v
    wide[item, o : o + 4 * GROUP] = tiles[slot, item, o : o + 4 * GROUP].astype(F32)
    return wide[item, pl.ds(o + side, GROUP, stride=4), :]


def inner_kernel(table, px, w, out_ref, buffers, tiles, wide, arrived):
    n = pl.program_id(0)
    slot = start_next(2 * BATCH, px, w, table, buffers, tiles, arrived)

    def steps(sums):
        def finish(pair):
            for place in range(2):
                rows = slice(16 * pair, 16 * pair + 16)
                out_ref[place, rows] = diagonal_sum(pltpu.matmul_pop(sums[pair][place]))

        for pair in range(BATCH):
            items = (2 * pair, 2 * pair + 1)
            for item in items:
                for copy in fetch(px, w, table, n, buffers, tiles, arrived, slot, item):
                    copy.wait()

            def strips(v):
                weight_a, weight_b = (
                    side_of(tiles, wide, slot, item, entry(table, n, 2 * item + 1), v) for item in items
                )
                joint = (weight_a * weight_b).astype(BF16)
                dense = slice(GROUP * v, GROUP * (v + 1))
                return [(buffers[slot, item, dense], joint) for item in items]

            strip_products(sums[pair], strips)
            if pair > 0:
                finish(pair - 1)
        finish(BATCH - 1)

    with_sums(steps)


def inner_sums(px, w):
    steps = len(INNER) // BATCH
    return pl.pallas_call(
        functools.partial(inner_kernel, INNER.reshape(steps, 4 * BATCH)),
        grid=(steps,),
        in_specs=[pl.BlockSpec(memory_space=pl.ANY)] * 2,
        out_specs=pl.BlockSpec((2, BATCH * 16, 256), lambda n: (0, n, 0)),
        scratch_shapes=[
            pltpu.VMEM((2, 2 * BATCH, CHUNKS, LANES), I32),
            pltpu.VMEM((2, 2 * BATCH, LINES, LANES), BF16),
            pltpu.VMEM((2 * BATCH, LINES, LANES), F32),
            pltpu.SemaphoreType.DMA((2, 2 * BATCH, 2)),
        ],
        out_shape=jax.ShapeDtypeStruct((2, len(INNER) * 16, 256), F32),
        compiler_params=pltpu.CompilerParams(vmem_limit_bytes=VMEM_BYTES),
        cost_estimate=pl.CostEstimate(
            flops=len(INNER) * 4 * 256 * 256 * 8192, bytes_accessed=30 << 20, transcendentals=0
        ),
    )(px, w)


def outer_kernel(
    table, px, w, below, above, left, out_ref, buffers, tiles, wide, arrived
):
    n = pl.program_id(0)
    slot = start_next(BATCH, px, w, table, buffers, tiles, arrived)

    def steps(sums):
        def finish(pair):
            own, other = (diagonal_sum(pltpu.matmul_pop(sums[pair][place])) for place in range(2))
            rows = slice(16 * pair, 16 * pair + 16)
            out_ref[0, rows] = jnp.where(n == 0, own, other)
            out_ref[1, rows] = jnp.where(n == 0, other, own)

        for pair in range(BATCH):
            for copy in fetch(px, w, table, n, buffers, tiles, arrived, slot, pair):
                copy.wait()

            def strips(v):
                dense = slice(GROUP * v, GROUP * (v + 1))

                def far(k):
                    return jnp.where(
                        n == 0, below[pair, k, dense],
                        jnp.where(n == 1, above[pair, k, dense], left[pair, k, dense]),
                    ).astype(F32)

                own = side_of(tiles, wide, slot, pair, entry(table, n, 2 * pair + 1), v)
                joint = (own * far(1)).astype(BF16)
                return (buffers[slot, pair, dense], joint), (far(0).astype(I32), joint)

            strip_products(sums[pair], strips)
            if pair > 0:
                finish(pair - 1)
        finish(BATCH - 1)

    with_sums(steps)


def outer_sums(px, w, below, above, left):
    count = len(OUTER)
    vmem = pl.BlockSpec(memory_space=pltpu.VMEM)
    return pl.pallas_call(
        functools.partial(outer_kernel, OUTER.reshape(count // BATCH, 2 * BATCH)),
        grid=(count // BATCH,),
        in_specs=[pl.BlockSpec(memory_space=pl.ANY)] * 2 + [vmem] * 3,
        out_specs=pl.BlockSpec((2, BATCH * 16, 256), lambda n: (0, n, 0)),
        scratch_shapes=[
            pltpu.VMEM((2, BATCH, CHUNKS, LANES), I32),
            pltpu.VMEM((2, BATCH, LINES, LANES), BF16),
            pltpu.VMEM((BATCH, LINES, LANES), F32),
            pltpu.SemaphoreType.DMA((2, BATCH, 2)),
        ],
        out_shape=jax.ShapeDtypeStruct((2, count * 16, 256), F32),
        compiler_params=pltpu.CompilerParams(vmem_limit_bytes=VMEM_BYTES),
        cost_estimate=pl.CostEstimate(
            flops=count * 4 * 256 * 256 * 8192, bytes_accessed=9 << 20, transcendentals=0
        ),
    )(px, w, below, above, left)


def pieces(x):
    high = x.astype(BF16)
    rest = x - high.astype(F32)
    middle = rest.astype(BF16)
    return high, middle, (rest - middle.astype(F32)).astype(BF16)


def apply(coefficients, x):
    exact = coefficients.astype(BF16)
    return jnp.dot(
        jnp.concatenate([exact] * 3, 1), jnp.concatenate(pieces(x), 0), preferred_element_type=F32
    )


def apply_right(x, coefficients):
    exact = coefficients.astype(BF16)
    return jnp.dot(
        jnp.concatenate(pieces(x), 1), jnp.concatenate([exact] * 3, 0), preferred_element_type=F32
    )


def pair_results(first, second):
    iota = lambda shape, dim: lax.broadcasted_iota(I32, shape, dim)
    difference = first - second
    within = (iota((256, LANES), 0) // GROUP <= iota((256, LANES), 1)) & (iota((256, LANES), 1) < 16)
    row, other = iota((256, 256), 0), iota((256, 256), 1)
    before = (row // 16 == other // 16) & (other < row)
    earlier = jnp.sum(apply(before.astype(F32), difference), axis=1, keepdims=True)
    cumulative = apply_right(difference, within.astype(F32)) + earlier
    size = jnp.where(iota((256, LANES), 1) < 16, jnp.abs(cumulative), 0.0)
    pair, member = iota((32, 256), 0), iota((32, 256), 1)
    mine = pair % 16 == member // 16
    heights = jnp.where(mine, jnp.where(pair < 16, 1, member % 16 * 16), 0).astype(F32)
    sums = apply(heights, jnp.concatenate([first, second, size], 1))
    lower = (iota((16, 256), 1) // GROUP).astype(F32) + 0.5
    reduce = lambda x: jnp.sum(x, axis=1, keepdims=True)
    total = reduce(sums[:16, :256])
    mean_first = reduce(sums[:16, :256] * lower + sums[16:, :256]) / total
    mean_second = reduce(sums[:16, 256:512] * lower + sums[16:, 256:512]) / total
    distance = reduce(sums[:16, 512:]) / total
    mismatch = (distance - jnp.abs(mean_first - mean_second)) / mismatch_scale
    confidence = 1.0 / (0.25 + mismatch * mismatch)
    offset = jnp.log(mean_second) - jnp.log(mean_first)
    number, lane = iota((16, LANES), 0), iota((16, LANES), 1)
    spread = jnp.where(number == lane, confidence, jnp.where(number == lane - 16, offset, 0.0))
    return jnp.sum(jnp.where(total > 0, spread, 0.0), axis=0, keepdims=True)


def results_kernel(inner, outer, out_ref):
    first, second = (jnp.concatenate([inner[k], outer[k]], 0) for k in range(2))
    out_ref[...] = jnp.broadcast_to(pair_results(first, second), out_ref.shape)


def results(inner, outer, devices):
    return pl.pallas_call(
        results_kernel,
        in_specs=[pl.BlockSpec(memory_space=pltpu.VMEM)] * 2,
        out_specs=pl.BlockSpec(memory_space=pltpu.VMEM),
        out_shape=jax.ShapeDtypeStruct((devices, LANES), F32),
    )(inner, outer)


def on_grid(gathered, height, count_y):
    devices = gathered.shape[0]
    slot = lax.broadcasted_iota(I32, (LANES, LANES), 0)
    lane = lax.broadcasted_iota(I32, (LANES, LANES), 1)
    c, odd, right = lane % 4, lane // 32 % 2, lane // 64 == 1
    offset_slots = 16 * odd
    edge = right & (c == 3)
    slots = [
        jnp.where(edge, 14, jnp.where(right, 4 + c, c)),
        jnp.where(edge, 15, jnp.where(right, 7 + c, jnp.where(c < 2, 10 + c, -100))),
        jnp.where(right | (c < 2), -100, 10 + c),
    ]
    choose = jnp.concatenate([(slot == s + offset_slots).astype(F32) for s in slots], 1)
    chosen = apply_right(gathered, choose)
    device = lax.broadcasted_iota(I32, (devices, LANES), 0)
    lane = lax.broadcasted_iota(I32, (devices, LANES), 1)
    shifted = ((lane // 64 == 1) & (lane % 4 == 3)).astype(I32)
    here = device // count_y == lane % 32 // 4 + shifted
    parts = [jnp.where(here, chosen[:, LANES * k : LANES * (k + 1)], 0.0) for k in range(3)]
    row = lax.broadcasted_iota(I32, (height, devices), 0)
    top = lax.broadcasted_iota(I32, (height, devices), 1) % count_y * 2
    place = jnp.concatenate([(row == top + k).astype(F32) for k in (0, 1, -1)], 1)
    return apply(place, jnp.concatenate(parts, 0))


def sweep_kernel(height, width, count_y, where_ref, gathered, adjacency, out_ref, links, gain_ref):
    grid = on_grid(gathered[...], height, count_y)
    links[...] = jnp.zeros_like(links)
    links[:, :, :width] = adjacency[...]
    row = lax.broadcasted_iota(I32, (height, LANES), 0)
    column = lax.broadcasted_iota(I32, (height, LANES), 1)
    below = (links[1] > 0) & (row < height - 1) & (column < width)
    beside = (links[0] > 0) & (column < width - 1)

    def lanes_of(k, present):
        values = grid if k == 0 else pltpu.roll(grid, LANES - 32 * k, 1)
        return jnp.where(present, values, 0.0)

    conf_down, off_down = lanes_of(0, below), lanes_of(1, below)
    conf_right, off_right = lanes_of(2, beside), lanes_of(3, beside)
    up = lambda a: pltpu.roll(a, 1, 0)
    down = lambda a: pltpu.roll(a, height - 1, 0)
    lefts = lambda a: pltpu.roll(a, 1, 1)
    rights = lambda a: pltpu.roll(a, LANES - 1, 1)
    conf_up, off_up = up(conf_down), -up(off_down)
    conf_left, off_left = lefts(conf_right), -lefts(off_right)
    scale = 1.0 / (anchor_weight + conf_up + conf_down + conf_left + conf_right)
    constant = scale * (
        conf_up * off_up + conf_down * off_down + conf_left * off_left + conf_right * off_right
    )
    a_up, a_down, a_left, a_right = (scale * a for a in (conf_up, conf_down, conf_left, conf_right))

    ones = a_up + a_down + a_left + a_right

    def mean(a):
        columns = jnp.sum(a, axis=0, keepdims=True)
        return jnp.sum(columns, axis=1, keepdims=True) * (1.0 / (height * width))

    def sweep(_, fresh):
        spread = (
            (a_up * up(fresh) + a_down * down(fresh))
            + (a_left * lefts(fresh) + a_right * rights(fresh))
            + constant
        )
        return spread - mean(fresh) * ones

    fresh = lax.fori_loop(0, ITERS - 1, sweep, constant, unroll=True)
    gain = fresh - mean(fresh)
    gain_ref[...] = pltpu.roll(gain, LANES - where_ref[1] * COLS, 1)
    out_ref[...] = gain_ref[pl.ds(where_ref[0] * ROWS, ROWS), :COLS]


def sweeps(gathered, adjacency, where):
    height, width = adjacency.shape[1:]
    return pl.pallas_call(
        functools.partial(sweep_kernel, height, width, height // ROWS),
        in_specs=[
            pl.BlockSpec(memory_space=pltpu.SMEM),
            pl.BlockSpec(memory_space=pltpu.VMEM),
            pl.BlockSpec(memory_space=pltpu.VMEM),
        ],
        out_specs=pl.BlockSpec(memory_space=pltpu.VMEM),
        out_shape=jax.ShapeDtypeStruct((ROWS, COLS), F32),
        scratch_shapes=[pltpu.VMEM((2, height, LANES), I32), pltpu.VMEM((height, LANES), F32)],
    )(where, gathered, adjacency)


def body(pixels, weights, adjacency):
    px = pixels.reshape(ROWS * COLS, 4, CHUNKS, LANES).transpose(0, 2, 1, 3)
    w = weights.reshape(ROWS * COLS, 4, CHUNKS, LANES).transpose(0, 2, 1, 3)
    w = w.reshape(ROWS * COLS, LINES, LANES)
    count_x, count_y = lax.axis_size("gx"), lax.axis_size("gy")
    ahead = lambda n: [(i, i + 1) for i in range(n - 1)]
    back = lambda n: [(i + 1, i) for i in range(n - 1)]
    below, above, left = packed(px, w)
    below = lax.ppermute(below, "gy", back(count_y))
    above = lax.ppermute(above, "gy", ahead(count_y))
    left = lax.ppermute(left, "gx", ahead(count_x))
    inner = inner_sums(px, w)
    outer = outer_sums(px, w, below, above, left)
    gathered = lax.all_to_all(results(inner, outer, count_x * count_y), ALL, 0, 0, tiled=True)
    where = jnp.stack([lax.axis_index("gy"), lax.axis_index("gx")]).astype(I32)
    return sweeps(gathered, adjacency, where)


def solution(mesh):
    return jax.shard_map(
        body,
        mesh=mesh,
        in_specs=(P("gy", "gx", None, None), P("gy", "gx", None, None), P()),
        out_specs=P("gy", "gx"),
        check_vma=False,
    )
```

```python
import functools

import jax
import jax.numpy as jnp
import numpy as np
from jax import lax
from jax.experimental import pallas as pl
from jax.experimental.pallas import tpu as pltpu
from jax.sharding import PartitionSpec as P

ITERS = 20
ROWS, COLS = 2, 4
CHUNKS, LANES = 1024, 128
LINES = 4 * CHUNKS
BATCH = 3
OUTER_BATCH = 2
GROUP = 16
ALL = ("gx", "gy")
F32, BF16, I32 = jnp.float32, jnp.bfloat16, jnp.int32

anchor_weight = 0.5
mismatch_scale = 8.0

INNER = np.array(
    [(c, 1, 4 + c, 0) for c in range(4)]
    + [(4 * r + c, 3, 4 * r + c + 1, 2) for r in range(2) for c in range(3)],
    np.int32,
)
SENT = (((0, 0), (1, 0)), ((6, 1), (7, 1)), ((3, 3), (7, 3)))
OUTER = np.array([(4, 1), (5, 1), (2, 0), (3, 0), (0, 2), (4, 2)], np.int32)


def one_hot_pair(bins, joint):
    upper = lax.shift_right_logical(bins, 4).astype(F32).astype(BF16)
    lower = (bins & 15).astype(F32).astype(BF16)
    zero, one = jnp.zeros((), BF16), jnp.ones((), BF16)
    left = [jnp.where(upper == BF16(k), joint, zero) for k in range(16)]
    right = [jnp.where(lower == BF16(k), one, zero) for k in range(16)]
    return jnp.concatenate(left, 0), jnp.concatenate(right, 0)


def diagonal_sum(product):
    column = lax.broadcasted_iota(I32, (GROUP, 256), 1) % GROUP
    row = lax.broadcasted_iota(I32, (GROUP, 256), 0)
    kept = jnp.where((column == row)[None], product.reshape(16, GROUP, 256), 0.0)
    return jnp.sum(kept, axis=1)


def strip_products(sums, strips):
    for part in range(CHUNKS // GROUP // 2):
        pairs = zip(*(strips(2 * part + half) for half in range(2)))
        for unit, halves in enumerate(pairs):
            left, right = zip(*(one_hot_pair(bins, joint) for bins, joint in halves))
            pltpu.matmul_push_rhs(jnp.concatenate(right, 1), part % 2, unit, transpose=True)
            pltpu.matmul_acc_lhs(sums[unit], jnp.concatenate(left, 1), load_staged_rhs=part % 2)


def with_sums(function):
    units = [pltpu.ACC(unit)((256, 256), F32) for _ in range(2) for unit in range(2)]
    pl.run_scoped(lambda *refs: function([refs[:2], refs[2:]]), *units)


def entry(table, step, column):
    values = [int(v) for v in table[:, column]]
    chosen = jnp.int32(values[0])
    for k in range(1, len(values)):
        if values[k] != values[k - 1]:
            chosen = jnp.where(step >= k, jnp.int32(values[k]), chosen)
    return chosen


def fetch(px, w, table, step, buffers, tiles, arrived, slot, item):
    tile, side = entry(table, step, 2 * item), entry(table, step, 2 * item + 1)
    return (
        pltpu.make_async_copy(px.at[tile, :, side, :], buffers.at[slot, item], arrived.at[slot, item, 0]),
        pltpu.make_async_copy(w.at[tile], tiles.at[slot, item], arrived.at[slot, item, 1]),
    )


def start_next(items, *refs):
    n, steps = pl.program_id(0), pl.num_programs(0)
    px, w, table, buffers, tiles, arrived = refs
    slot = lax.rem(n, 2)

    def start(step, place):
        for item in range(items):
            for copy in fetch(px, w, table, step, buffers, tiles, arrived, place, item):
                copy.start()

    @pl.when(n == 0)
    def _():
        start(0, 0)

    @pl.when(n + 1 < steps)
    def _():
        start(n + 1, 1 - slot)

    return slot


def side_of(tiles, wide, place, room, side, v):
    o = 4 * GROUP * v
    wide[room, o : o + 4 * GROUP] = tiles[place, o : o + 4 * GROUP].astype(F32)
    return wide[room, pl.ds(o + side, GROUP, stride=4), :]


def pack_kernel(
    px, w, below_ref, above_ref, left_ref, sums_ref, pixels, tiles, wide, px_arrived, w_arrived
):
    jobs = [(out, n) + SENT[k][n] for k, out in enumerate((below_ref, above_ref, left_ref)) for n in range(2)]
    first = [tuple(int(v) for v in INNER[0, 2 * k : 2 * k + 2]) for k in range(2)]
    strips = first + [job[2:] for job in jobs]
    needed = list(dict.fromkeys(tile for tile, _ in strips))
    w_copies = [
        pltpu.make_async_copy(w.at[tile], tiles.at[k], w_arrived.at[k]) for k, tile in enumerate(needed)
    ]
    px_copies = [
        pltpu.make_async_copy(px.at[tile, :, side, :], pixels.at[k], px_arrived.at[k])
        for k, (tile, side) in enumerate(strips)
    ]
    for copy in px_copies[:2] + w_copies + px_copies[2:]:
        copy.start()
    for copy in px_copies[:2] + w_copies[:2]:
        copy.wait()

    def first_pair(sums):
        def strips_at(v):
            weight_a, weight_b = (side_of(tiles, wide, k, k, first[k][1], v) for k in range(2))
            joint = (weight_a * weight_b).astype(BF16)
            dense = slice(GROUP * v, GROUP * (v + 1))
            return [(pixels[k, dense], joint) for k in range(2)]

        strip_products(sums[0], strips_at)
        for place in range(2):
            sums_ref[place] = diagonal_sum(pltpu.matmul_pop(sums[0][place]))

    with_sums(first_pair)
    for k, tile in enumerate(needed):
        mine = [job for job in jobs if job[2] == tile]
        if k >= 2:
            w_copies[k].wait()
        if mine:
            wide[k % 2] = tiles[k].astype(F32)
        for out, n, _, side in mine:
            out[n, 1] = wide[k % 2, pl.ds(side, CHUNKS, stride=4), :].astype(BF16)
    for k, (out, n, _, _) in enumerate(jobs):
        px_copies[2 + k].wait()
        out[n, 0] = pixels[2 + k].astype(F32).astype(BF16)


def packed(px, w):
    strips = jax.ShapeDtypeStruct((2, 2, CHUNKS, LANES), BF16)
    tiles = len({t for pair in SENT for t, _ in pair} | {int(INNER[0, 0]), int(INNER[0, 2])})
    vmem = pl.BlockSpec(memory_space=pltpu.VMEM)
    return pl.pallas_call(
        pack_kernel,
        in_specs=[pl.BlockSpec(memory_space=pl.ANY)] * 2,
        out_specs=[vmem] * 4,
        out_shape=[strips] * 3 + [jax.ShapeDtypeStruct((2, 16, 256), F32)],
        scratch_shapes=[
            pltpu.VMEM((8, CHUNKS, LANES), I32),
            pltpu.VMEM((tiles, LINES, LANES), BF16),
            pltpu.VMEM((2, LINES, LANES), F32),
            pltpu.SemaphoreType.DMA((8,)),
            pltpu.SemaphoreType.DMA((tiles,)),
        ],
        compiler_params=pltpu.CompilerParams(vmem_limit_bytes=48 << 20),
        cost_estimate=pl.CostEstimate(flops=1 << 30, bytes_accessed=10 << 20, transcendentals=0),
    )(px, w)


def inner_kernel(table, px, w, out_ref, buffers, tiles, wide, arrived):
    n = pl.program_id(0)
    slot = start_next(2 * BATCH, px, w, table, buffers, tiles, arrived)

    def steps(sums):
        def finish(pair):
            for place in range(2):
                rows = slice(16 * pair, 16 * pair + 16)
                out_ref[place, rows] = diagonal_sum(pltpu.matmul_pop(sums[pair % 2][place]))

        for pair in range(BATCH):
            items = (2 * pair, 2 * pair + 1)
            for item in items:
                for copy in fetch(px, w, table, n, buffers, tiles, arrived, slot, item):
                    copy.wait()

            def strips(v):
                weight_a, weight_b = (
                    side_of(tiles.at[slot], wide, item, item % 2, entry(table, n, 2 * item + 1), v)
                    for item in items
                )
                joint = (weight_a * weight_b).astype(BF16)
                dense = slice(GROUP * v, GROUP * (v + 1))
                return [(buffers[slot, item, dense], joint) for item in items]

            strip_products(sums[pair % 2], strips)
            if pair > 0:
                finish(pair - 1)
        finish(BATCH - 1)

    with_sums(steps)


def inner_sums(px, w):
    count = len(INNER) - 1
    steps = count // BATCH
    return pl.pallas_call(
        functools.partial(inner_kernel, INNER[1:].reshape(steps, 4 * BATCH)),
        grid=(steps,),
        in_specs=[pl.BlockSpec(memory_space=pl.ANY)] * 2,
        out_specs=pl.BlockSpec((2, BATCH * 16, 256), lambda n: (0, n, 0)),
        scratch_shapes=[
            pltpu.VMEM((2, 2 * BATCH, CHUNKS, LANES), I32),
            pltpu.VMEM((2, 2 * BATCH, LINES, LANES), BF16),
            pltpu.VMEM((2, LINES, LANES), F32),
            pltpu.SemaphoreType.DMA((2, 2 * BATCH, 2)),
        ],
        out_shape=jax.ShapeDtypeStruct((2, count * 16, 256), F32),
        compiler_params=pltpu.CompilerParams(vmem_limit_bytes=48 << 20),
        cost_estimate=pl.CostEstimate(
            flops=count * 4 * 256 * 256 * 8192, bytes_accessed=30 << 20, transcendentals=0
        ),
    )(px, w)


def outer_kernel(
    table, px, w, below, above, left, start, inner, out_ref, buffers, tiles, wide, arrived
):
    n = pl.program_id(0)
    slot = start_next(OUTER_BATCH, px, w, table, buffers, tiles, arrived)

    def steps(sums):
        def finish(pair):
            own, other = (diagonal_sum(pltpu.matmul_pop(sums[pair % 2][place])) for place in range(2))
            at = len(INNER) + OUTER_BATCH * n + pair
            rows = pl.ds(pl.multiple_of(at * 16, 16), 16)
            out_ref[0, rows] = jnp.where(n == 0, own, other)
            out_ref[1, rows] = jnp.where(n == 0, other, own)

        for pair in range(OUTER_BATCH):
            for copy in fetch(px, w, table, n, buffers, tiles, arrived, slot, pair):
                copy.wait()

            def strips(v):
                dense = slice(GROUP * v, GROUP * (v + 1))

                def far(k):
                    return jnp.where(
                        n == 0, below[pair, k, dense],
                        jnp.where(n == 1, above[pair, k, dense], left[pair, k, dense]),
                    ).astype(F32)

                own = side_of(tiles.at[slot], wide, pair, pair, entry(table, n, 2 * pair + 1), v)
                joint = (own * far(1)).astype(BF16)
                return (buffers[slot, pair, dense], joint), (far(0).astype(I32), joint)

            strip_products(sums[pair % 2], strips)
            if pair > 0:
                finish(pair - 1)
        finish(OUTER_BATCH - 1)

    with_sums(steps)

    @pl.when(n == 0)
    def _():
        out_ref[:, :16] = start[...]
        out_ref[:, 16 : len(INNER) * 16] = inner[...]


def all_sums(px, w, below, above, left, start, inner):
    count = len(OUTER)
    vmem = pl.BlockSpec(memory_space=pltpu.VMEM)
    return pl.pallas_call(
        functools.partial(outer_kernel, OUTER.reshape(count // OUTER_BATCH, 2 * OUTER_BATCH)),
        grid=(count // OUTER_BATCH,),
        in_specs=[pl.BlockSpec(memory_space=pl.ANY)] * 2 + [vmem] * 5,
        out_specs=vmem,
        scratch_shapes=[
            pltpu.VMEM((2, OUTER_BATCH, CHUNKS, LANES), I32),
            pltpu.VMEM((2, OUTER_BATCH, LINES, LANES), BF16),
            pltpu.VMEM((OUTER_BATCH, LINES, LANES), F32),
            pltpu.SemaphoreType.DMA((2, OUTER_BATCH, 2)),
        ],
        out_shape=jax.ShapeDtypeStruct((2, (len(INNER) + count) * 16, 256), F32),
        compiler_params=pltpu.CompilerParams(vmem_limit_bytes=48 << 20),
        cost_estimate=pl.CostEstimate(
            flops=count * 4 * 256 * 256 * 8192, bytes_accessed=9 << 20, transcendentals=0
        ),
    )(px, w, below, above, left, start, inner)


def pieces(x):
    high = x.astype(BF16)
    rest = x - high.astype(F32)
    middle = rest.astype(BF16)
    return high, middle, (rest - middle.astype(F32)).astype(BF16)


def apply(coefficients, x):
    exact = coefficients.astype(BF16)
    return jnp.dot(
        jnp.concatenate([exact] * 3, 1), jnp.concatenate(pieces(x), 0), preferred_element_type=F32
    )


def apply_right(x, coefficients):
    exact = coefficients.astype(BF16)
    return jnp.dot(
        jnp.concatenate(pieces(x), 1), jnp.concatenate([exact] * 3, 0), preferred_element_type=F32
    )


def pair_results(first, second):
    iota = lambda shape, dim: lax.broadcasted_iota(I32, shape, dim)
    difference = first - second
    within = (iota((256, LANES), 0) // GROUP <= iota((256, LANES), 1)) & (iota((256, LANES), 1) < 16)
    row, other = iota((256, 256), 0), iota((256, 256), 1)
    before = (row // 16 == other // 16) & (other < row)
    earlier = jnp.sum(apply(before.astype(F32), difference), axis=1, keepdims=True)
    cumulative = apply_right(difference, within.astype(F32)) + earlier
    size = jnp.where(iota((256, LANES), 1) < 16, jnp.abs(cumulative), 0.0)
    pair, member = iota((32, 256), 0), iota((32, 256), 1)
    mine = pair % 16 == member // 16
    heights = jnp.where(mine, jnp.where(pair < 16, 1, member % 16 * 16), 0).astype(F32)
    sums = apply(heights, jnp.concatenate([first, second, size], 1))
    lower = (iota((16, 256), 1) // GROUP).astype(F32) + 0.5
    reduce = lambda x: jnp.sum(x, axis=1, keepdims=True)
    total = reduce(sums[:16, :256])
    mean_first = reduce(sums[:16, :256] * lower + sums[16:, :256]) / total
    mean_second = reduce(sums[:16, 256:512] * lower + sums[16:, 256:512]) / total
    distance = reduce(sums[:16, 512:]) / total
    mismatch = (distance - jnp.abs(mean_first - mean_second)) / mismatch_scale
    confidence = 1.0 / (0.25 + mismatch * mismatch)
    offset = jnp.log(mean_second) - jnp.log(mean_first)
    number, lane = iota((16, LANES), 0), iota((16, LANES), 1)
    spread = jnp.where(number == lane, confidence, jnp.where(number == lane - 16, offset, 0.0))
    return jnp.sum(jnp.where(total > 0, spread, 0.0), axis=0, keepdims=True)


def results_kernel(sums, out_ref):
    out_ref[...] = jnp.broadcast_to(pair_results(sums[0], sums[1]), out_ref.shape)


def results(sums, devices):
    return pl.pallas_call(
        results_kernel,
        in_specs=[pl.BlockSpec(memory_space=pltpu.VMEM)],
        out_specs=pl.BlockSpec(memory_space=pltpu.VMEM),
        out_shape=jax.ShapeDtypeStruct((devices, LANES), F32),
    )(sums)


def on_grid(gathered, height, count_y):
    devices = gathered.shape[0]
    slot = lax.broadcasted_iota(I32, (LANES, LANES), 0)
    lane = lax.broadcasted_iota(I32, (LANES, LANES), 1)
    c, odd, right = lane % 4, lane // 32 % 2, lane // 64 == 1
    offset_slots = 16 * odd
    edge = right & (c == 3)
    slots = [
        jnp.where(edge, 14, jnp.where(right, 4 + c, c)),
        jnp.where(edge, 15, jnp.where(right, 7 + c, jnp.where(c < 2, 10 + c, -100))),
        jnp.where(right | (c < 2), -100, 10 + c),
    ]
    choose = jnp.concatenate([(slot == s + offset_slots).astype(F32) for s in slots], 1)
    chosen = apply_right(gathered, choose)
    device = lax.broadcasted_iota(I32, (devices, LANES), 0)
    lane = lax.broadcasted_iota(I32, (devices, LANES), 1)
    shifted = ((lane // 64 == 1) & (lane % 4 == 3)).astype(I32)
    here = device // count_y == lane % 32 // 4 + shifted
    parts = [jnp.where(here, chosen[:, LANES * k : LANES * (k + 1)], 0.0) for k in range(3)]
    row = lax.broadcasted_iota(I32, (height, devices), 0)
    top = lax.broadcasted_iota(I32, (height, devices), 1) % count_y * 2
    place = jnp.concatenate([(row == top + k).astype(F32) for k in (0, 1, -1)], 1)
    return apply(place, jnp.concatenate(parts, 0))


def sweep_kernel(height, width, count_y, where_ref, gathered, adjacency, out_ref, held, links, gain_ref, arrived):
    copy = pltpu.make_async_copy(adjacency, held, arrived)
    copy.start()
    grid = on_grid(gathered[...], height, count_y)
    links[...] = jnp.zeros_like(links)
    copy.wait()
    links[:, :, :width] = held[...]
    row = lax.broadcasted_iota(I32, (height, LANES), 0)
    column = lax.broadcasted_iota(I32, (height, LANES), 1)
    below = (links[1] > 0) & (row < height - 1) & (column < width)
    beside = (links[0] > 0) & (column < width - 1)

    def lanes_of(k, present):
        values = grid if k == 0 else pltpu.roll(grid, LANES - 32 * k, 1)
        return jnp.where(present, values, 0.0)

    conf_down, off_down = lanes_of(0, below), lanes_of(1, below)
    conf_right, off_right = lanes_of(2, beside), lanes_of(3, beside)
    up = lambda a: pltpu.roll(a, 1, 0)
    down = lambda a: pltpu.roll(a, height - 1, 0)
    lefts = lambda a: pltpu.roll(a, 1, 1)
    rights = lambda a: pltpu.roll(a, LANES - 1, 1)
    conf_up, off_up = up(conf_down), -up(off_down)
    conf_left, off_left = lefts(conf_right), -lefts(off_right)
    scale = 1.0 / (anchor_weight + conf_up + conf_down + conf_left + conf_right)
    constant = scale * (
        conf_up * off_up + conf_down * off_down + conf_left * off_left + conf_right * off_right
    )
    a_up, a_down, a_left, a_right = (scale * a for a in (conf_up, conf_down, conf_left, conf_right))

    ones = a_up + a_down + a_left + a_right
    columns = down(a_up) + up(a_down) + rights(a_left) + lefts(a_right)

    def mean(a):
        by_column = jnp.sum(a, axis=0, keepdims=True)
        return jnp.sum(by_column, axis=1, keepdims=True) * (1.0 / (height * width))

    mean_constant, mean_ones = mean(constant), mean(ones)

    def sweep(_, state):
        fresh, average = state
        spread = (
            (a_up * up(fresh) + a_down * down(fresh))
            + (a_left * lefts(fresh) + a_right * rights(fresh))
            + constant
        )
        later = mean(columns * fresh) + (mean_constant - average * mean_ones)
        return spread - average * ones, later

    fresh, average = lax.fori_loop(0, ITERS - 1, sweep, (constant, mean_constant), unroll=True)
    gain = fresh - average
    gain_ref[...] = pltpu.roll(gain, LANES - where_ref[1] * COLS, 1)
    out_ref[...] = gain_ref[pl.ds(where_ref[0] * ROWS, ROWS), :COLS]


def sweeps(gathered, adjacency, where):
    height, width = adjacency.shape[1:]
    return pl.pallas_call(
        functools.partial(sweep_kernel, height, width, height // ROWS),
        in_specs=[
            pl.BlockSpec(memory_space=pltpu.SMEM),
            pl.BlockSpec(memory_space=pltpu.VMEM),
            pl.BlockSpec(memory_space=pl.ANY),
        ],
        out_specs=pl.BlockSpec(memory_space=pltpu.VMEM),
        out_shape=jax.ShapeDtypeStruct((ROWS, COLS), F32),
        scratch_shapes=[
            pltpu.VMEM(adjacency.shape, I32),
            pltpu.VMEM((2, height, LANES), I32),
            pltpu.VMEM((height, LANES), F32),
            pltpu.SemaphoreType.DMA,
        ],
        compiler_params=pltpu.CompilerParams(vmem_limit_bytes=56 << 20),
    )(where, gathered, adjacency)


def body(pixels, weights, adjacency):
    px = pixels.reshape(ROWS * COLS, 4, CHUNKS, LANES).transpose(0, 2, 1, 3)
    w = weights.reshape(ROWS * COLS, 4, CHUNKS, LANES).transpose(0, 2, 1, 3)
    w = w.reshape(ROWS * COLS, LINES, LANES)
    count_x, count_y = lax.axis_size("gx"), lax.axis_size("gy")
    ahead = lambda n: [(i, i + 1) for i in range(n - 1)]
    back = lambda n: [(i + 1, i) for i in range(n - 1)]
    below, above, left, start = packed(px, w)
    below = lax.ppermute(below, "gy", back(count_y))
    above = lax.ppermute(above, "gy", ahead(count_y))
    left = lax.ppermute(left, "gx", ahead(count_x))
    inner = inner_sums(px, w)
    sums = all_sums(px, w, below, above, left, start, inner)
    gathered = lax.all_to_all(results(sums, count_x * count_y), ALL, 0, 0, tiled=True)
    where = jnp.stack([lax.axis_index("gy"), lax.axis_index("gx")]).astype(I32)
    return sweeps(gathered, adjacency, where)


def solution(mesh):
    return jax.shard_map(
        body,
        mesh=mesh,
        in_specs=(P("gy", "gx", None, None), P("gy", "gx", None, None), P()),
        out_specs=P("gy", "gx"),
        check_vma=False,
    )
```

```python
import functools

import jax
import jax.numpy as jnp
import numpy as np
from jax import lax
from jax.experimental import pallas as pl
from jax.experimental.pallas import tpu as pltpu
from jax.sharding import PartitionSpec as P

ITERS = 20
ROWS, COLS = 2, 4
CHUNKS, LANES = 1024, 128
LINES = 4 * CHUNKS
BATCH = 2
OUTER_BATCH = 2
GROUP = 16
ALL = ("gx", "gy")
F32, BF16, I32 = jnp.float32, jnp.bfloat16, jnp.int32

anchor_weight = 0.5
mismatch_scale = 8.0

INNER = np.array(
    [(c, 1, 4 + c, 0) for c in range(4)]
    + [(4 * r + c, 3, 4 * r + c + 1, 2) for r in range(2) for c in range(3)],
    np.int32,
)
SENT = (((0, 0), (1, 0)), ((6, 1), (7, 1)), ((3, 3), (7, 3)))
OUTER = np.array([(4, 1), (5, 1), (2, 0), (3, 0), (0, 2), (4, 2)], np.int32)


def one_hot_pair(bins, joint):
    upper = lax.shift_right_logical(bins, 4).astype(F32).astype(BF16)
    lower = (bins & 15).astype(F32).astype(BF16)
    zero, one = jnp.zeros((), BF16), jnp.ones((), BF16)
    left = [jnp.where(upper == BF16(k), joint, zero) for k in range(16)]
    right = [jnp.where(lower == BF16(k), one, zero) for k in range(16)]
    return jnp.concatenate(left, 0), jnp.concatenate(right, 0)


def diagonal_sum(product):
    column = lax.broadcasted_iota(I32, (GROUP, 256), 1) % GROUP
    row = lax.broadcasted_iota(I32, (GROUP, 256), 0)
    kept = jnp.where((column == row)[None], product.reshape(16, GROUP, 256), 0.0)
    return jnp.sum(kept, axis=1)


def strip_products(sums, strips):
    for part in range(CHUNKS // GROUP // 2):
        pairs = zip(*(strips(2 * part + half) for half in range(2)))
        for unit, halves in enumerate(pairs):
            left, right = zip(*(one_hot_pair(bins, joint) for bins, joint in halves))
            pltpu.matmul_push_rhs(jnp.concatenate(right, 1), part % 2, unit, transpose=True)
            pltpu.matmul_acc_lhs(sums[unit], jnp.concatenate(left, 1), load_staged_rhs=part % 2)


def with_sums(function):
    units = [pltpu.ACC(unit)((256, 256), F32) for _ in range(2) for unit in range(2)]
    pl.run_scoped(lambda *refs: function([refs[:2], refs[2:]]), *units)


def entry(table, step, column):
    values = [int(v) for v in table[:, column]]
    chosen = jnp.int32(values[0])
    for k in range(1, len(values)):
        if values[k] != values[k - 1]:
            chosen = jnp.where(step >= k, jnp.int32(values[k]), chosen)
    return chosen


def fetch(px, w, table, step, buffers, tiles, arrived, slot, item):
    tile, side = entry(table, step, 2 * item), entry(table, step, 2 * item + 1)
    return (
        pltpu.make_async_copy(px.at[tile, :, side, :], buffers.at[slot, item], arrived.at[slot, item, 0]),
        pltpu.make_async_copy(w.at[tile], tiles.at[slot, item], arrived.at[slot, item, 1]),
    )


def start_next(items, *refs):
    n, steps = pl.program_id(0), pl.num_programs(0)
    px, w, table, buffers, tiles, arrived = refs
    slot = lax.rem(n, 2)

    def start(step, place):
        for item in range(items):
            for copy in fetch(px, w, table, step, buffers, tiles, arrived, place, item):
                copy.start()

    @pl.when(n == 0)
    def _():
        start(0, 0)

    @pl.when(n + 1 < steps)
    def _():
        start(n + 1, 1 - slot)

    return slot


def side_of(tiles, wide, place, room, side, v):
    o = 4 * GROUP * v
    wide[room, o : o + 4 * GROUP] = tiles[place, o : o + 4 * GROUP].astype(F32)
    return wide[room, pl.ds(o + side, GROUP, stride=4), :]


def pack_kernel(px, w, below_ref, above_ref, left_ref, pixels, tiles, wide, px_arrived, w_arrived):
    jobs = [(out, n) + SENT[k][n] for k, out in enumerate((below_ref, above_ref, left_ref)) for n in range(2)]
    needed = sorted({job[2] for job in jobs}, key=[job[2] for job in jobs].index)
    w_copies = [
        pltpu.make_async_copy(w.at[tile], tiles.at[k], w_arrived.at[k]) for k, tile in enumerate(needed)
    ]
    px_copies = [
        pltpu.make_async_copy(px.at[job[2], :, job[3], :], pixels.at[k], px_arrived.at[k])
        for k, job in enumerate(jobs)
    ]
    for copy in w_copies + px_copies:
        copy.start()
    for k, tile in enumerate(needed):
        w_copies[k].wait()
        wide[k % 2] = tiles[k].astype(F32)
        for out, n, _, side in (job for job in jobs if job[2] == tile):
            out[n, 1] = wide[k % 2, pl.ds(side, CHUNKS, stride=4), :].astype(BF16)
    for k, (out, n, _, _) in enumerate(jobs):
        px_copies[k].wait()
        out[n, 0] = pixels[k].astype(F32).astype(BF16)


def packed(px, w):
    strips = jax.ShapeDtypeStruct((2, 2, CHUNKS, LANES), BF16)
    vmem = pl.BlockSpec(memory_space=pltpu.VMEM)
    return pl.pallas_call(
        pack_kernel,
        in_specs=[pl.BlockSpec(memory_space=pl.ANY)] * 2,
        out_specs=[vmem] * 3,
        out_shape=[strips] * 3,
        scratch_shapes=[
            pltpu.VMEM((6, CHUNKS, LANES), I32),
            pltpu.VMEM((5, LINES, LANES), BF16),
            pltpu.VMEM((2, LINES, LANES), F32),
            pltpu.SemaphoreType.DMA((6,)),
            pltpu.SemaphoreType.DMA((5,)),
        ],
        compiler_params=pltpu.CompilerParams(vmem_limit_bytes=48 << 20),
        cost_estimate=pl.CostEstimate(flops=1 << 20, bytes_accessed=8 << 20, transcendentals=0),
    )(px, w)


def inner_kernel(table, px, w, out_ref, buffers, tiles, wide, arrived):
    n = pl.program_id(0)
    slot = start_next(2 * BATCH, px, w, table, buffers, tiles, arrived)

    def steps(sums):
        def finish(pair):
            for place in range(2):
                rows = slice(16 * pair, 16 * pair + 16)
                out_ref[place, rows] = diagonal_sum(pltpu.matmul_pop(sums[pair % 2][place]))

        for pair in range(BATCH):
            items = (2 * pair, 2 * pair + 1)
            for item in items:
                for copy in fetch(px, w, table, n, buffers, tiles, arrived, slot, item):
                    copy.wait()

            def strips(v):
                weight_a, weight_b = (
                    side_of(tiles.at[slot], wide, item, item % 2, entry(table, n, 2 * item + 1), v)
                    for item in items
                )
                joint = (weight_a * weight_b).astype(BF16)
                dense = slice(GROUP * v, GROUP * (v + 1))
                return [(buffers[slot, item, dense], joint) for item in items]

            strip_products(sums[pair % 2], strips)
            if pair > 0:
                finish(pair - 1)
        finish(BATCH - 1)

    with_sums(steps)


def inner_sums(px, w):
    count = len(INNER)
    steps = count // BATCH
    return pl.pallas_call(
        functools.partial(inner_kernel, INNER.reshape(steps, 4 * BATCH)),
        grid=(steps,),
        in_specs=[pl.BlockSpec(memory_space=pl.ANY)] * 2,
        out_specs=pl.BlockSpec((2, BATCH * 16, 256), lambda n: (0, n, 0)),
        scratch_shapes=[
            pltpu.VMEM((2, 2 * BATCH, CHUNKS, LANES), I32),
            pltpu.VMEM((2, 2 * BATCH, LINES, LANES), BF16),
            pltpu.VMEM((2, LINES, LANES), F32),
            pltpu.SemaphoreType.DMA((2, 2 * BATCH, 2)),
        ],
        out_shape=jax.ShapeDtypeStruct((2, count * 16, 256), F32),
        compiler_params=pltpu.CompilerParams(vmem_limit_bytes=48 << 20),
        cost_estimate=pl.CostEstimate(
            flops=count * 4 * 256 * 256 * 8192, bytes_accessed=30 << 20, transcendentals=0
        ),
    )(px, w)


def outer_kernel(
    table, px, w, below, above, left, inner, out_ref, buffers, tiles, wide, arrived, received, staged
):
    n = pl.program_id(0)
    for step, source in enumerate((below, above, left)):

        @pl.when(n == step)
        def _(source=source):
            pltpu.make_async_copy(source, received, staged).start()

    slot = start_next(OUTER_BATCH, px, w, table, buffers, tiles, arrived)
    pltpu.make_async_copy(below, received, staged).wait()

    def steps(sums):
        def finish(pair):
            own, other = (diagonal_sum(pltpu.matmul_pop(sums[pair % 2][place])) for place in range(2))
            at = len(INNER) + OUTER_BATCH * n + pair
            rows = pl.ds(pl.multiple_of(at * 16, 16), 16)
            out_ref[0, rows] = jnp.where(n == 0, own, other)
            out_ref[1, rows] = jnp.where(n == 0, other, own)

        for pair in range(OUTER_BATCH):
            for copy in fetch(px, w, table, n, buffers, tiles, arrived, slot, pair):
                copy.wait()

            def strips(v):
                dense = slice(GROUP * v, GROUP * (v + 1))

                own = side_of(tiles.at[slot], wide, pair, pair, entry(table, n, 2 * pair + 1), v)
                joint = (own * received[pair, 1, dense].astype(F32)).astype(BF16)
                far = received[pair, 0, dense].astype(F32).astype(I32)
                return (buffers[slot, pair, dense], joint), (far, joint)

            strip_products(sums[pair % 2], strips)
            if pair > 0:
                finish(pair - 1)
        finish(OUTER_BATCH - 1)

    with_sums(steps)

    @pl.when(n == 0)
    def _():
        out_ref[:, : len(INNER) * 16] = inner[...]


def all_sums(px, w, below, above, left, inner):
    count = len(OUTER)
    vmem = pl.BlockSpec(memory_space=pltpu.VMEM)
    return pl.pallas_call(
        functools.partial(outer_kernel, OUTER.reshape(count // OUTER_BATCH, 2 * OUTER_BATCH)),
        grid=(count // OUTER_BATCH,),
        in_specs=[pl.BlockSpec(memory_space=pl.ANY)] * 2 + [vmem] * 4,
        out_specs=vmem,
        scratch_shapes=[
            pltpu.VMEM((2, OUTER_BATCH, CHUNKS, LANES), I32),
            pltpu.VMEM((2, OUTER_BATCH, LINES, LANES), BF16),
            pltpu.VMEM((OUTER_BATCH, LINES, LANES), F32),
            pltpu.SemaphoreType.DMA((2, OUTER_BATCH, 2)),
            pltpu.VMEM(below.shape, BF16),
            pltpu.SemaphoreType.DMA,
        ],
        out_shape=jax.ShapeDtypeStruct((2, (len(INNER) + count) * 16, 256), F32),
        compiler_params=pltpu.CompilerParams(vmem_limit_bytes=48 << 20),
        cost_estimate=pl.CostEstimate(
            flops=count * 4 * 256 * 256 * 8192, bytes_accessed=9 << 20, transcendentals=0
        ),
    )(px, w, below, above, left, inner)


def pieces(x):
    high = x.astype(BF16)
    rest = x - high.astype(F32)
    middle = rest.astype(BF16)
    return high, middle, (rest - middle.astype(F32)).astype(BF16)


def apply(coefficients, x):
    exact = coefficients.astype(BF16)
    return jnp.dot(
        jnp.concatenate([exact] * 3, 1), jnp.concatenate(pieces(x), 0), preferred_element_type=F32
    )


def apply_right(x, coefficients):
    exact = coefficients.astype(BF16)
    return jnp.dot(
        jnp.concatenate(pieces(x), 1), jnp.concatenate([exact] * 3, 0), preferred_element_type=F32
    )


def pair_results(first, second):
    iota = lambda shape, dim: lax.broadcasted_iota(I32, shape, dim)
    difference = first - second
    within = (iota((256, LANES), 0) // GROUP <= iota((256, LANES), 1)) & (iota((256, LANES), 1) < 16)
    row, other = iota((256, 256), 0), iota((256, 256), 1)
    before = (row // 16 == other // 16) & (other < row)
    earlier = jnp.sum(apply(before.astype(F32), difference), axis=1, keepdims=True)
    cumulative = apply_right(difference, within.astype(F32)) + earlier
    size = jnp.where(iota((256, LANES), 1) < 16, jnp.abs(cumulative), 0.0)
    pair, member = iota((32, 256), 0), iota((32, 256), 1)
    mine = pair % 16 == member // 16
    heights = jnp.where(mine, jnp.where(pair < 16, 1, member % 16 * 16), 0).astype(F32)
    sums = apply(heights, jnp.concatenate([first, second, size], 1))
    lower = (iota((16, 256), 1) // GROUP).astype(F32) + 0.5
    reduce = lambda x: jnp.sum(x, axis=1, keepdims=True)
    total = reduce(sums[:16, :256])
    mean_first = reduce(sums[:16, :256] * lower + sums[16:, :256]) / total
    mean_second = reduce(sums[:16, 256:512] * lower + sums[16:, 256:512]) / total
    distance = reduce(sums[:16, 512:]) / total
    mismatch = (distance - jnp.abs(mean_first - mean_second)) / mismatch_scale
    confidence = 1.0 / (0.25 + mismatch * mismatch)
    offset = jnp.log(mean_second) - jnp.log(mean_first)
    number, lane = iota((16, LANES), 0), iota((16, LANES), 1)
    spread = jnp.where(number == lane, confidence, jnp.where(number == lane - 16, offset, 0.0))
    return jnp.sum(jnp.where(total > 0, spread, 0.0), axis=0, keepdims=True)


def results_kernel(sums, out_ref):
    out_ref[...] = jnp.broadcast_to(pair_results(sums[0], sums[1]), out_ref.shape)


def results(sums, devices):
    return pl.pallas_call(
        results_kernel,
        in_specs=[pl.BlockSpec(memory_space=pltpu.VMEM)],
        out_specs=pl.BlockSpec(memory_space=pltpu.VMEM),
        out_shape=jax.ShapeDtypeStruct((devices, LANES), F32),
        compiler_params=pltpu.CompilerParams(vmem_limit_bytes=16 << 20),
    )(sums)


def on_grid(gathered, height, count_y):
    devices = gathered.shape[0]
    slot = lax.broadcasted_iota(I32, (LANES, LANES), 0)
    lane = lax.broadcasted_iota(I32, (LANES, LANES), 1)
    c, odd, right = lane % 4, lane // 32 % 2, lane // 64 == 1
    offset_slots = 16 * odd
    edge = right & (c == 3)
    slots = [
        jnp.where(edge, 14, jnp.where(right, 4 + c, c)),
        jnp.where(edge, 15, jnp.where(right, 7 + c, jnp.where(c < 2, 10 + c, -100))),
        jnp.where(right | (c < 2), -100, 10 + c),
    ]
    choose = jnp.concatenate([(slot == s + offset_slots).astype(F32) for s in slots], 1)
    chosen = apply_right(gathered, choose)
    device = lax.broadcasted_iota(I32, (devices, LANES), 0)
    lane = lax.broadcasted_iota(I32, (devices, LANES), 1)
    shifted = ((lane // 64 == 1) & (lane % 4 == 3)).astype(I32)
    here = device // count_y == lane % 32 // 4 + shifted
    parts = [jnp.where(here, chosen[:, LANES * k : LANES * (k + 1)], 0.0) for k in range(3)]
    row = lax.broadcasted_iota(I32, (height, devices), 0)
    top = lax.broadcasted_iota(I32, (height, devices), 1) % count_y * 2
    place = jnp.concatenate([(row == top + k).astype(F32) for k in (0, 1, -1)], 1)
    return apply(place, jnp.concatenate(parts, 0))


def sweep_kernel(height, width, count_y, where_ref, gathered, adjacency, out_ref, held, links, gain_ref, arrived):
    copy = pltpu.make_async_copy(adjacency, held, arrived)
    copy.start()
    grid = on_grid(gathered[...], height, count_y)
    links[...] = jnp.zeros_like(links)
    copy.wait()
    links[:, :, :width] = held[...]
    row = lax.broadcasted_iota(I32, (height, LANES), 0)
    column = lax.broadcasted_iota(I32, (height, LANES), 1)
    below = (links[1] > 0) & (row < height - 1) & (column < width)
    beside = (links[0] > 0) & (column < width - 1)

    def lanes_of(k, present):
        values = grid if k == 0 else pltpu.roll(grid, LANES - 32 * k, 1)
        return jnp.where(present, values, 0.0)

    conf_down, off_down = lanes_of(0, below), lanes_of(1, below)
    conf_right, off_right = lanes_of(2, beside), lanes_of(3, beside)
    up = lambda a: pltpu.roll(a, 1, 0)
    down = lambda a: pltpu.roll(a, height - 1, 0)
    lefts = lambda a: pltpu.roll(a, 1, 1)
    rights = lambda a: pltpu.roll(a, LANES - 1, 1)
    conf_up, off_up = up(conf_down), -up(off_down)
    conf_left, off_left = lefts(conf_right), -lefts(off_right)
    scale = 1.0 / (anchor_weight + conf_up + conf_down + conf_left + conf_right)
    constant = scale * (
        conf_up * off_up + conf_down * off_down + conf_left * off_left + conf_right * off_right
    )
    a_up, a_down, a_left, a_right = (scale * a for a in (conf_up, conf_down, conf_left, conf_right))

    ones = a_up + a_down + a_left + a_right
    columns = down(a_up) + up(a_down) + rights(a_left) + lefts(a_right)

    def mean(a):
        by_column = jnp.sum(a, axis=0, keepdims=True)
        return jnp.sum(by_column, axis=1, keepdims=True) * (1.0 / (height * width))

    mean_constant, mean_ones = mean(constant), mean(ones)

    def sweep(_, state):
        fresh, average = state
        spread = (
            (a_up * up(fresh) + a_down * down(fresh))
            + (a_left * lefts(fresh) + a_right * rights(fresh))
            + constant
        )
        later = mean(columns * fresh) + (mean_constant - average * mean_ones)
        return spread - average * ones, later

    fresh, average = lax.fori_loop(0, ITERS - 1, sweep, (constant, mean_constant), unroll=True)
    gain = fresh - average
    gain_ref[...] = pltpu.roll(gain, LANES - where_ref[1] * COLS, 1)
    out_ref[...] = gain_ref[pl.ds(where_ref[0] * ROWS, ROWS), :COLS]


def sweeps(gathered, adjacency, where):
    height, width = adjacency.shape[1:]
    return pl.pallas_call(
        functools.partial(sweep_kernel, height, width, height // ROWS),
        in_specs=[
            pl.BlockSpec(memory_space=pltpu.SMEM),
            pl.BlockSpec(memory_space=pltpu.VMEM),
            pl.BlockSpec(memory_space=pl.ANY),
        ],
        out_specs=pl.BlockSpec(memory_space=pltpu.VMEM),
        out_shape=jax.ShapeDtypeStruct((ROWS, COLS), F32),
        scratch_shapes=[
            pltpu.VMEM(adjacency.shape, I32),
            pltpu.VMEM((2, height, LANES), I32),
            pltpu.VMEM((height, LANES), F32),
            pltpu.SemaphoreType.DMA,
        ],
        compiler_params=pltpu.CompilerParams(vmem_limit_bytes=8 << 20),
    )(where, gathered, adjacency)


def body(pixels, weights, adjacency):
    px = pixels.reshape(ROWS * COLS, 4, CHUNKS, LANES).transpose(0, 2, 1, 3)
    w = weights.reshape(ROWS * COLS, 4, CHUNKS, LANES).transpose(0, 2, 1, 3)
    w = w.reshape(ROWS * COLS, LINES, LANES)
    count_x, count_y = lax.axis_size("gx"), lax.axis_size("gy")
    ahead = lambda n: [(i, i + 1) for i in range(n - 1)]
    back = lambda n: [(i + 1, i) for i in range(n - 1)]
    below, above, left = packed(px, w)
    below = lax.ppermute(below, "gy", back(count_y))
    above = lax.ppermute(above, "gy", ahead(count_y))
    left = lax.ppermute(left, "gx", ahead(count_x))
    inner = inner_sums(px, w)
    sums = all_sums(px, w, below, above, left, inner)
    gathered = lax.all_to_all(results(sums, count_x * count_y), ALL, 0, 0, tiled=True)
    where = jnp.stack([lax.axis_index("gy"), lax.axis_index("gx")]).astype(I32)
    return sweeps(gathered, adjacency, where)


def solution(mesh):
    return jax.shard_map(
        body,
        mesh=mesh,
        in_specs=(P("gy", "gx", None, None), P("gy", "gx", None, None), P()),
        out_specs=P("gy", "gx"),
        check_vma=False,
    )
```

```python
import functools

import jax
import jax.numpy as jnp
import numpy as np
from jax import lax
from jax.experimental import pallas as pl
from jax.experimental.pallas import tpu as pltpu
from jax.sharding import PartitionSpec as P

ITERS = 20
ROWS, COLS = 2, 4
CHUNKS, LANES = 1024, 128
LINES = 4 * CHUNKS
BATCH = 2
OUTER_BATCH = 2
GROUP = 16
ALL = ("gx", "gy")
F32, BF16, I32 = jnp.float32, jnp.bfloat16, jnp.int32

anchor_weight = 0.5
mismatch_scale = 8.0

INNER = np.array(
    [(c, 1, 4 + c, 0) for c in range(4)]
    + [(4 * r + c, 3, 4 * r + c + 1, 2) for r in range(2) for c in range(3)],
    np.int32,
)
SENT = (((0, 0), (1, 0)), ((6, 1), (7, 1)), ((3, 3), (7, 3)))
OUTER = np.array([(4, 1), (5, 1), (2, 0), (3, 0), (0, 2), (4, 2)], np.int32)


def one_hot_pair(bins, joint):
    upper = lax.shift_right_logical(bins, 4).astype(F32).astype(BF16)
    lower = (bins & 15).astype(F32).astype(BF16)
    zero, one = jnp.zeros((), BF16), jnp.ones((), BF16)
    left = [jnp.where(upper == BF16(k), joint, zero) for k in range(16)]
    right = [jnp.where(lower == BF16(k), one, zero) for k in range(16)]
    return jnp.concatenate(left, 0), jnp.concatenate(right, 0)


def diagonal_sum(product):
    column = lax.broadcasted_iota(I32, (GROUP, 256), 1) % GROUP
    row = lax.broadcasted_iota(I32, (GROUP, 256), 0)
    kept = jnp.where((column == row)[None], product.reshape(16, GROUP, 256), 0.0)
    return jnp.sum(kept, axis=1)


def strip_products(sums, strips):
    for part in range(CHUNKS // GROUP // 2):
        pairs = zip(*(strips(2 * part + half) for half in range(2)))
        for unit, halves in enumerate(pairs):
            left, right = zip(*(one_hot_pair(bins, joint) for bins, joint in halves))
            pltpu.matmul_push_rhs(jnp.concatenate(right, 1), part % 2, unit, transpose=True)
            pltpu.matmul_acc_lhs(sums[unit], jnp.concatenate(left, 1), load_staged_rhs=part % 2)


def with_sums(function):
    units = [pltpu.ACC(unit)((256, 256), F32) for _ in range(2) for unit in range(2)]
    pl.run_scoped(lambda *refs: function([refs[:2], refs[2:]]), *units)


def entry(table, step, column):
    values = [int(v) for v in table[:, column]]
    chosen = jnp.int32(values[0])
    for k in range(1, len(values)):
        if values[k] != values[k - 1]:
            chosen = jnp.where(step >= k, jnp.int32(values[k]), chosen)
    return chosen


def fetch(px, w, table, step, buffers, tiles, arrived, slot, item):
    tile, side = entry(table, step, 2 * item), entry(table, step, 2 * item + 1)
    return (
        pltpu.make_async_copy(px.at[tile, :, side, :], buffers.at[slot, item], arrived.at[slot, item, 0]),
        pltpu.make_async_copy(w.at[tile], tiles.at[slot, item], arrived.at[slot, item, 1]),
    )


def start_next(items, *refs):
    n, steps = pl.program_id(0), pl.num_programs(0)
    px, w, table, buffers, tiles, arrived = refs
    slot = lax.rem(n, 2)

    def start(step, place):
        for item in range(items):
            for copy in fetch(px, w, table, step, buffers, tiles, arrived, place, item):
                copy.start()

    @pl.when(n == 0)
    def _():
        start(0, 0)

    @pl.when(n + 1 < steps)
    def _():
        start(n + 1, 1 - slot)

    return slot


def side_of(tiles, wide, place, room, side, v):
    o = 4 * GROUP * v
    wide[room, o : o + 4 * GROUP] = tiles[place, o : o + 4 * GROUP].astype(F32)
    return wide[room, pl.ds(o + side, GROUP, stride=4), :]


def pack_kernel(px, w, below_ref, above_ref, left_ref, pixels, tiles, wide, px_arrived, w_arrived):
    jobs = [(out, n) + SENT[k][n] for k, out in enumerate((below_ref, above_ref, left_ref)) for n in range(2)]
    needed = sorted({job[2] for job in jobs}, key=[job[2] for job in jobs].index)
    w_copies = [
        pltpu.make_async_copy(w.at[tile], tiles.at[k], w_arrived.at[k]) for k, tile in enumerate(needed)
    ]
    px_copies = [
        pltpu.make_async_copy(px.at[job[2], :, job[3], :], pixels.at[k], px_arrived.at[k])
        for k, job in enumerate(jobs)
    ]
    for copy in w_copies + px_copies:
        copy.start()
    for k, tile in enumerate(needed):
        w_copies[k].wait()
        wide[k % 2] = tiles[k].astype(F32)
        for out, n, _, side in (job for job in jobs if job[2] == tile):
            out[n, 1] = wide[k % 2, pl.ds(side, CHUNKS, stride=4), :].astype(BF16)
    for k, (out, n, _, _) in enumerate(jobs):
        px_copies[k].wait()
        out[n, 0] = pixels[k].astype(F32).astype(BF16)


def packed(px, w):
    strips = jax.ShapeDtypeStruct((2, 2, CHUNKS, LANES), BF16)
    vmem = pl.BlockSpec(memory_space=pltpu.VMEM)
    return pl.pallas_call(
        pack_kernel,
        in_specs=[pl.BlockSpec(memory_space=pl.ANY)] * 2,
        out_specs=[vmem] * 3,
        out_shape=[strips] * 3,
        scratch_shapes=[
            pltpu.VMEM((6, CHUNKS, LANES), I32),
            pltpu.VMEM((5, LINES, LANES), BF16),
            pltpu.VMEM((2, LINES, LANES), F32),
            pltpu.SemaphoreType.DMA((6,)),
            pltpu.SemaphoreType.DMA((5,)),
        ],
        compiler_params=pltpu.CompilerParams(vmem_limit_bytes=48 << 20),
        cost_estimate=pl.CostEstimate(flops=1 << 20, bytes_accessed=8 << 20, transcendentals=0),
    )(px, w)


def inner_kernel(table, px, w, out_ref, buffers, tiles, wide, arrived):
    n = pl.program_id(0)
    slot = start_next(2 * BATCH, px, w, table, buffers, tiles, arrived)

    def steps(sums):
        def finish(pair):
            for place in range(2):
                rows = slice(16 * pair, 16 * pair + 16)
                out_ref[place, rows] = diagonal_sum(pltpu.matmul_pop(sums[pair % 2][place]))

        for pair in range(BATCH):
            items = (2 * pair, 2 * pair + 1)
            for item in items:
                for copy in fetch(px, w, table, n, buffers, tiles, arrived, slot, item):
                    copy.wait()

            def strips(v):
                weight_a, weight_b = (
                    side_of(tiles.at[slot], wide, item, item % 2, entry(table, n, 2 * item + 1), v)
                    for item in items
                )
                joint = (weight_a * weight_b).astype(BF16)
                dense = slice(GROUP * v, GROUP * (v + 1))
                return [(buffers[slot, item, dense], joint) for item in items]

            strip_products(sums[pair % 2], strips)
            if pair > 0:
                finish(pair - 1)
        finish(BATCH - 1)

    with_sums(steps)


def inner_sums(px, w):
    count = len(INNER)
    steps = count // BATCH
    return pl.pallas_call(
        functools.partial(inner_kernel, INNER.reshape(steps, 4 * BATCH)),
        grid=(steps,),
        in_specs=[pl.BlockSpec(memory_space=pl.ANY)] * 2,
        out_specs=pl.BlockSpec((2, BATCH * 16, 256), lambda n: (0, n, 0)),
        scratch_shapes=[
            pltpu.VMEM((2, 2 * BATCH, CHUNKS, LANES), I32),
            pltpu.VMEM((2, 2 * BATCH, LINES, LANES), BF16),
            pltpu.VMEM((2, LINES, LANES), F32),
            pltpu.SemaphoreType.DMA((2, 2 * BATCH, 2)),
        ],
        out_shape=jax.ShapeDtypeStruct((2, count * 16, 256), F32),
        compiler_params=pltpu.CompilerParams(vmem_limit_bytes=48 << 20),
        cost_estimate=pl.CostEstimate(
            flops=count * 4 * 256 * 256 * 8192, bytes_accessed=30 << 20, transcendentals=0
        ),
    )(px, w)


def outer_kernel(
    table, px, w, below, above, left, inner, out_ref, buffers, tiles, wide, arrived, received, staged
):
    n = pl.program_id(0)
    def stage(source, place):
        return pltpu.make_async_copy(source, received.at[place], staged.at[place])

    @pl.when(n == 0)
    def _():
        stage(below, 0).start()
        stage(above, 1).start()

    @pl.when(n == 1)
    def _():
        stage(left, 0).start()

    slot = start_next(OUTER_BATCH, px, w, table, buffers, tiles, arrived)
    stage(below, slot).wait()

    def steps(sums):
        def finish(pair):
            own, other = (diagonal_sum(pltpu.matmul_pop(sums[pair % 2][place])) for place in range(2))
            at = len(INNER) + OUTER_BATCH * n + pair
            rows = pl.ds(pl.multiple_of(at * 16, 16), 16)
            out_ref[0, rows] = jnp.where(n == 0, own, other)
            out_ref[1, rows] = jnp.where(n == 0, other, own)

        for pair in range(OUTER_BATCH):
            for copy in fetch(px, w, table, n, buffers, tiles, arrived, slot, pair):
                copy.wait()

            def strips(v):
                dense = slice(GROUP * v, GROUP * (v + 1))

                own = side_of(tiles.at[slot], wide, pair, pair, entry(table, n, 2 * pair + 1), v)
                joint = (own * received[slot, pair, 1, dense].astype(F32)).astype(BF16)
                far = received[slot, pair, 0, dense].astype(F32).astype(I32)
                return (buffers[slot, pair, dense], joint), (far, joint)

            strip_products(sums[pair % 2], strips)
            if pair > 0:
                finish(pair - 1)
        finish(OUTER_BATCH - 1)

    with_sums(steps)

    @pl.when(n == 0)
    def _():
        out_ref[:, : len(INNER) * 16] = inner[...]


def all_sums(px, w, below, above, left, inner):
    count = len(OUTER)
    vmem = pl.BlockSpec(memory_space=pltpu.VMEM)
    return pl.pallas_call(
        functools.partial(outer_kernel, OUTER.reshape(count // OUTER_BATCH, 2 * OUTER_BATCH)),
        grid=(count // OUTER_BATCH,),
        in_specs=[pl.BlockSpec(memory_space=pl.ANY)] * 2 + [vmem] * 4,
        out_specs=vmem,
        scratch_shapes=[
            pltpu.VMEM((2, OUTER_BATCH, CHUNKS, LANES), I32),
            pltpu.VMEM((2, OUTER_BATCH, LINES, LANES), BF16),
            pltpu.VMEM((OUTER_BATCH, LINES, LANES), F32),
            pltpu.SemaphoreType.DMA((2, OUTER_BATCH, 2)),
            pltpu.VMEM((2,) + below.shape, BF16),
            pltpu.SemaphoreType.DMA((2,)),
        ],
        out_shape=jax.ShapeDtypeStruct((2, (len(INNER) + count) * 16, 256), F32),
        compiler_params=pltpu.CompilerParams(vmem_limit_bytes=48 << 20),
        cost_estimate=pl.CostEstimate(
            flops=count * 4 * 256 * 256 * 8192, bytes_accessed=9 << 20, transcendentals=0
        ),
    )(px, w, below, above, left, inner)


def pieces(x):
    high = x.astype(BF16)
    rest = x - high.astype(F32)
    middle = rest.astype(BF16)
    return high, middle, (rest - middle.astype(F32)).astype(BF16)


def apply(coefficients, x):
    exact = coefficients.astype(BF16)
    return jnp.dot(
        jnp.concatenate([exact] * 3, 1), jnp.concatenate(pieces(x), 0), preferred_element_type=F32
    )


def apply_right(x, coefficients):
    exact = coefficients.astype(BF16)
    return jnp.dot(
        jnp.concatenate(pieces(x), 1), jnp.concatenate([exact] * 3, 0), preferred_element_type=F32
    )


def pair_results(first, second):
    iota = lambda shape, dim: lax.broadcasted_iota(I32, shape, dim)
    difference = first - second
    within = (iota((256, LANES), 0) // GROUP <= iota((256, LANES), 1)) & (iota((256, LANES), 1) < 16)
    row, other = iota((256, 256), 0), iota((256, 256), 1)
    before = (row // 16 == other // 16) & (other < row)
    earlier = jnp.sum(apply(before.astype(F32), difference), axis=1, keepdims=True)
    cumulative = apply_right(difference, within.astype(F32)) + earlier
    size = jnp.where(iota((256, LANES), 1) < 16, jnp.abs(cumulative), 0.0)
    pair, member = iota((32, 256), 0), iota((32, 256), 1)
    mine = pair % 16 == member // 16
    heights = jnp.where(mine, jnp.where(pair < 16, 1, member % 16 * 16), 0).astype(F32)
    sums = apply(heights, jnp.concatenate([first, second, size], 1))
    lower = (iota((16, 256), 1) // GROUP).astype(F32) + 0.5
    reduce = lambda x: jnp.sum(x, axis=1, keepdims=True)
    total = reduce(sums[:16, :256])
    mean_first = reduce(sums[:16, :256] * lower + sums[16:, :256]) / total
    mean_second = reduce(sums[:16, 256:512] * lower + sums[16:, 256:512]) / total
    distance = reduce(sums[:16, 512:]) / total
    mismatch = (distance - jnp.abs(mean_first - mean_second)) / mismatch_scale
    confidence = 1.0 / (0.25 + mismatch * mismatch)
    offset = jnp.log(mean_second) - jnp.log(mean_first)
    number, lane = iota((16, LANES), 0), iota((16, LANES), 1)
    spread = jnp.where(number == lane, confidence, jnp.where(number == lane - 16, offset, 0.0))
    return jnp.sum(jnp.where(total > 0, spread, 0.0), axis=0, keepdims=True)


def results_kernel(sums, out_ref):
    out_ref[...] = jnp.broadcast_to(pair_results(sums[0], sums[1]), out_ref.shape)


def results(sums, devices):
    return pl.pallas_call(
        results_kernel,
        in_specs=[pl.BlockSpec(memory_space=pltpu.VMEM)],
        out_specs=pl.BlockSpec(memory_space=pltpu.VMEM),
        out_shape=jax.ShapeDtypeStruct((devices, LANES), F32),
        compiler_params=pltpu.CompilerParams(vmem_limit_bytes=16 << 20),
    )(sums)


def on_grid(gathered, height, count_y):
    devices = gathered.shape[0]
    slot = lax.broadcasted_iota(I32, (LANES, LANES), 0)
    lane = lax.broadcasted_iota(I32, (LANES, LANES), 1)
    c, odd, right = lane % 4, lane // 32 % 2, lane // 64 == 1
    offset_slots = 16 * odd
    edge = right & (c == 3)
    slots = [
        jnp.where(edge, 14, jnp.where(right, 4 + c, c)),
        jnp.where(edge, 15, jnp.where(right, 7 + c, jnp.where(c < 2, 10 + c, -100))),
        jnp.where(right | (c < 2), -100, 10 + c),
    ]
    choose = jnp.concatenate([(slot == s + offset_slots).astype(F32) for s in slots], 1)
    chosen = apply_right(gathered, choose)
    device = lax.broadcasted_iota(I32, (devices, LANES), 0)
    lane = lax.broadcasted_iota(I32, (devices, LANES), 1)
    shifted = ((lane // 64 == 1) & (lane % 4 == 3)).astype(I32)
    here = device // count_y == lane % 32 // 4 + shifted
    parts = [jnp.where(here, chosen[:, LANES * k : LANES * (k + 1)], 0.0) for k in range(3)]
    row = lax.broadcasted_iota(I32, (height, devices), 0)
    top = lax.broadcasted_iota(I32, (height, devices), 1) % count_y * 2
    place = jnp.concatenate([(row == top + k).astype(F32) for k in (0, 1, -1)], 1)
    return apply(place, jnp.concatenate(parts, 0))


def sweep_kernel(height, width, count_y, where_ref, gathered, adjacency, out_ref, held, links, gain_ref, arrived):
    copy = pltpu.make_async_copy(adjacency, held, arrived)
    copy.start()
    grid = on_grid(gathered[...], height, count_y)
    links[...] = jnp.zeros_like(links)
    copy.wait()
    links[:, :, :width] = held[...]
    row = lax.broadcasted_iota(I32, (height, LANES), 0)
    column = lax.broadcasted_iota(I32, (height, LANES), 1)
    below = (links[1] > 0) & (row < height - 1) & (column < width)
    beside = (links[0] > 0) & (column < width - 1)

    def lanes_of(k, present):
        values = grid if k == 0 else pltpu.roll(grid, LANES - 32 * k, 1)
        return jnp.where(present, values, 0.0)

    conf_down, off_down = lanes_of(0, below), lanes_of(1, below)
    conf_right, off_right = lanes_of(2, beside), lanes_of(3, beside)
    up = lambda a: pltpu.roll(a, 1, 0)
    down = lambda a: pltpu.roll(a, height - 1, 0)
    lefts = lambda a: pltpu.roll(a, 1, 1)
    rights = lambda a: pltpu.roll(a, LANES - 1, 1)
    conf_up, off_up = up(conf_down), -up(off_down)
    conf_left, off_left = lefts(conf_right), -lefts(off_right)
    scale = 1.0 / (anchor_weight + conf_up + conf_down + conf_left + conf_right)
    constant = scale * (
        conf_up * off_up + conf_down * off_down + conf_left * off_left + conf_right * off_right
    )
    a_up, a_down, a_left, a_right = (scale * a for a in (conf_up, conf_down, conf_left, conf_right))

    ones = a_up + a_down + a_left + a_right
    columns = down(a_up) + up(a_down) + rights(a_left) + lefts(a_right)

    def mean(a):
        by_column = jnp.sum(a, axis=0, keepdims=True)
        return jnp.sum(by_column, axis=1, keepdims=True) * (1.0 / (height * width))

    mean_constant, mean_ones = mean(constant), mean(ones)

    def sweep(_, state):
        fresh, average = state
        spread = (
            (a_up * up(fresh) + a_down * down(fresh))
            + (a_left * lefts(fresh) + a_right * rights(fresh))
            + constant
        )
        later = mean(columns * fresh) + (mean_constant - average * mean_ones)
        return spread - average * ones, later

    fresh, average = lax.fori_loop(0, ITERS - 1, sweep, (constant, mean_constant), unroll=True)
    gain = fresh - average
    gain_ref[...] = pltpu.roll(gain, LANES - where_ref[1] * COLS, 1)
    out_ref[...] = gain_ref[pl.ds(where_ref[0] * ROWS, ROWS), :COLS]


def sweeps(gathered, adjacency, where):
    height, width = adjacency.shape[1:]
    return pl.pallas_call(
        functools.partial(sweep_kernel, height, width, height // ROWS),
        in_specs=[
            pl.BlockSpec(memory_space=pltpu.SMEM),
            pl.BlockSpec(memory_space=pltpu.VMEM),
            pl.BlockSpec(memory_space=pl.ANY),
        ],
        out_specs=pl.BlockSpec(memory_space=pltpu.VMEM),
        out_shape=jax.ShapeDtypeStruct((ROWS, COLS), F32),
        scratch_shapes=[
            pltpu.VMEM(adjacency.shape, I32),
            pltpu.VMEM((2, height, LANES), I32),
            pltpu.VMEM((height, LANES), F32),
            pltpu.SemaphoreType.DMA,
        ],
        compiler_params=pltpu.CompilerParams(vmem_limit_bytes=8 << 20),
    )(where, gathered, adjacency)


def body(pixels, weights, adjacency):
    px = pixels.reshape(ROWS * COLS, 4, CHUNKS, LANES).transpose(0, 2, 1, 3)
    w = weights.reshape(ROWS * COLS, 4, CHUNKS, LANES).transpose(0, 2, 1, 3)
    w = w.reshape(ROWS * COLS, LINES, LANES)
    count_x, count_y = lax.axis_size("gx"), lax.axis_size("gy")
    ahead = lambda n: [(i, i + 1) for i in range(n - 1)]
    back = lambda n: [(i + 1, i) for i in range(n - 1)]
    below, above, left = packed(px, w)
    below = lax.ppermute(below, "gy", back(count_y))
    above = lax.ppermute(above, "gy", ahead(count_y))
    left = lax.ppermute(left, "gx", ahead(count_x))
    inner = inner_sums(px, w)
    sums = all_sums(px, w, below, above, left, inner)
    gathered = lax.all_to_all(results(sums, count_x * count_y), ALL, 0, 0, tiled=True)
    where = jnp.stack([lax.axis_index("gy"), lax.axis_index("gx")]).astype(I32)
    return sweeps(gathered, adjacency, where)


def solution(mesh):
    return jax.shard_map(
        body,
        mesh=mesh,
        in_specs=(P("gy", "gx", None, None), P("gy", "gx", None, None), P()),
        out_specs=P("gy", "gx"),
        check_vma=False,
    )
```

```python
import functools

import jax
import jax.numpy as jnp
import numpy as np
from jax import lax
from jax.experimental import pallas as pl
from jax.experimental.pallas import tpu as pltpu
from jax.sharding import PartitionSpec as P

ITERS = 20
ROWS, COLS = 2, 4
CHUNKS, LANES = 1024, 128
LINES = 4 * CHUNKS
BATCH = 2
OUTER_BATCH = 6
GROUP = 16
ALL = ("gx", "gy")
F32, BF16, I32 = jnp.float32, jnp.bfloat16, jnp.int32

anchor_weight = 0.5
mismatch_scale = 8.0

INNER = np.array(
    [(c, 1, 4 + c, 0) for c in range(4)]
    + [(4 * r + c, 3, 4 * r + c + 1, 2) for r in range(2) for c in range(3)],
    np.int32,
)
SENT = (((0, 0), (1, 0)), ((6, 1), (7, 1)), ((3, 3), (7, 3)))
OUTER = np.array([(4, 1), (5, 1), (2, 0), (3, 0), (0, 2), (4, 2)], np.int32)


def one_hot_pair(bins, joint):
    upper = lax.shift_right_logical(bins, 4).astype(F32).astype(BF16)
    lower = (bins & 15).astype(F32).astype(BF16)
    zero, one = jnp.zeros((), BF16), jnp.ones((), BF16)
    left = [jnp.where(upper == BF16(k), joint, zero) for k in range(16)]
    right = [jnp.where(lower == BF16(k), one, zero) for k in range(16)]
    return jnp.concatenate(left, 0), jnp.concatenate(right, 0)


def diagonal_sum(product):
    column = lax.broadcasted_iota(I32, (GROUP, 256), 1) % GROUP
    row = lax.broadcasted_iota(I32, (GROUP, 256), 0)
    kept = jnp.where((column == row)[None], product.reshape(16, GROUP, 256), 0.0)
    return jnp.sum(kept, axis=1)


def strip_products(sums, strips):
    for part in range(CHUNKS // GROUP // 2):
        pairs = zip(*(strips(2 * part + half) for half in range(2)))
        for unit, halves in enumerate(pairs):
            left, right = zip(*(one_hot_pair(bins, joint) for bins, joint in halves))
            pltpu.matmul_push_rhs(jnp.concatenate(right, 1), part % 2, unit, transpose=True)
            pltpu.matmul_acc_lhs(sums[unit], jnp.concatenate(left, 1), load_staged_rhs=part % 2)


def with_sums(function):
    units = [pltpu.ACC(unit)((256, 256), F32) for _ in range(2) for unit in range(2)]
    pl.run_scoped(lambda *refs: function([refs[:2], refs[2:]]), *units)


def entry(table, step, column):
    values = [int(v) for v in table[:, column]]
    chosen = jnp.int32(values[0])
    for k in range(1, len(values)):
        if values[k] != values[k - 1]:
            chosen = jnp.where(step >= k, jnp.int32(values[k]), chosen)
    return chosen


def fetch(px, w, table, step, buffers, tiles, arrived, slot, item):
    tile, side = entry(table, step, 2 * item), entry(table, step, 2 * item + 1)
    return (
        pltpu.make_async_copy(px.at[tile, :, side, :], buffers.at[slot, item], arrived.at[slot, item, 0]),
        pltpu.make_async_copy(w.at[tile], tiles.at[slot, item], arrived.at[slot, item, 1]),
    )


def start_next(items, *refs):
    n, steps = pl.program_id(0), pl.num_programs(0)
    px, w, table, buffers, tiles, arrived = refs
    slot = lax.rem(n, 2)

    def start(step, place):
        for item in range(items):
            for copy in fetch(px, w, table, step, buffers, tiles, arrived, place, item):
                copy.start()

    @pl.when(n == 0)
    def _():
        start(0, 0)

    @pl.when(n + 1 < steps)
    def _():
        start(n + 1, 1 - slot)

    return slot


def side_of(tiles, wide, place, room, side, v):
    o = 4 * GROUP * v
    wide[room, o : o + 4 * GROUP] = tiles[place, o : o + 4 * GROUP].astype(F32)
    return wide[room, pl.ds(o + side, GROUP, stride=4), :]


def pack_kernel(px, w, below_ref, above_ref, left_ref, pixels, tiles, wide, px_arrived, w_arrived):
    jobs = [(out, n) + SENT[k][n] for k, out in enumerate((below_ref, above_ref, left_ref)) for n in range(2)]
    needed = sorted({job[2] for job in jobs}, key=[job[2] for job in jobs].index)
    w_copies = [
        pltpu.make_async_copy(w.at[tile], tiles.at[k], w_arrived.at[k]) for k, tile in enumerate(needed)
    ]
    px_copies = [
        pltpu.make_async_copy(px.at[job[2], :, job[3], :], pixels.at[k], px_arrived.at[k])
        for k, job in enumerate(jobs)
    ]
    for copy in w_copies + px_copies:
        copy.start()
    for k, tile in enumerate(needed):
        w_copies[k].wait()
        wide[k % 2] = tiles[k].astype(F32)
        for out, n, _, side in (job for job in jobs if job[2] == tile):
            out[n, 1] = wide[k % 2, pl.ds(side, CHUNKS, stride=4), :].astype(BF16)
    for k, (out, n, _, _) in enumerate(jobs):
        px_copies[k].wait()
        out[n, 0] = pixels[k].astype(F32).astype(BF16)


def packed(px, w):
    strips = jax.ShapeDtypeStruct((2, 2, CHUNKS, LANES), BF16)
    vmem = pl.BlockSpec(memory_space=pltpu.VMEM)
    return pl.pallas_call(
        pack_kernel,
        in_specs=[pl.BlockSpec(memory_space=pl.ANY)] * 2,
        out_specs=[vmem] * 3,
        out_shape=[strips] * 3,
        scratch_shapes=[
            pltpu.VMEM((6, CHUNKS, LANES), I32),
            pltpu.VMEM((5, LINES, LANES), BF16),
            pltpu.VMEM((2, LINES, LANES), F32),
            pltpu.SemaphoreType.DMA((6,)),
            pltpu.SemaphoreType.DMA((5,)),
        ],
        compiler_params=pltpu.CompilerParams(vmem_limit_bytes=48 << 20),
        cost_estimate=pl.CostEstimate(flops=1 << 20, bytes_accessed=8 << 20, transcendentals=0),
    )(px, w)


def inner_kernel(table, px, w, out_ref, buffers, tiles, wide, arrived):
    n = pl.program_id(0)
    slot = start_next(2 * BATCH, px, w, table, buffers, tiles, arrived)

    def steps(sums):
        def finish(pair):
            for place in range(2):
                rows = slice(16 * pair, 16 * pair + 16)
                out_ref[place, rows] = diagonal_sum(pltpu.matmul_pop(sums[pair % 2][place]))

        for pair in range(BATCH):
            items = (2 * pair, 2 * pair + 1)
            for item in items:
                for copy in fetch(px, w, table, n, buffers, tiles, arrived, slot, item):
                    copy.wait()

            def strips(v):
                weight_a, weight_b = (
                    side_of(tiles.at[slot], wide, item, item % 2, entry(table, n, 2 * item + 1), v)
                    for item in items
                )
                joint = (weight_a * weight_b).astype(BF16)
                dense = slice(GROUP * v, GROUP * (v + 1))
                return [(buffers[slot, item, dense], joint) for item in items]

            strip_products(sums[pair % 2], strips)
            if pair > 0:
                finish(pair - 1)
        finish(BATCH - 1)

    with_sums(steps)


def inner_sums(px, w):
    count = len(INNER)
    steps = count // BATCH
    return pl.pallas_call(
        functools.partial(inner_kernel, INNER.reshape(steps, 4 * BATCH)),
        grid=(steps,),
        in_specs=[pl.BlockSpec(memory_space=pl.ANY)] * 2,
        out_specs=pl.BlockSpec((2, BATCH * 16, 256), lambda n: (0, n, 0)),
        scratch_shapes=[
            pltpu.VMEM((2, 2 * BATCH, CHUNKS, LANES), I32),
            pltpu.VMEM((2, 2 * BATCH, LINES, LANES), BF16),
            pltpu.VMEM((2, LINES, LANES), F32),
            pltpu.SemaphoreType.DMA((2, 2 * BATCH, 2)),
        ],
        out_shape=jax.ShapeDtypeStruct((2, count * 16, 256), F32),
        compiler_params=pltpu.CompilerParams(vmem_limit_bytes=48 << 20),
        cost_estimate=pl.CostEstimate(
            flops=count * 4 * 256 * 256 * 8192, bytes_accessed=30 << 20, transcendentals=0
        ),
    )(px, w)


def outer_kernel(
    table, px, w, below, above, left, inner, out_ref, buffers, tiles, wide, arrived
):
    n = pl.program_id(0)
    slot = start_next(OUTER_BATCH, px, w, table, buffers, tiles, arrived)

    def steps(sums):
        def finish(pair):
            own, other = (diagonal_sum(pltpu.matmul_pop(sums[pair % 2][place])) for place in range(2))
            at = len(INNER) + OUTER_BATCH * n + pair
            rows = pl.ds(pl.multiple_of(at * 16, 16), 16)
            out_ref[0, rows] = own if pair < 2 else other
            out_ref[1, rows] = other if pair < 2 else own

        for pair in range(OUTER_BATCH):
            for copy in fetch(px, w, table, n, buffers, tiles, arrived, slot, pair):
                copy.wait()

            def strips(v):
                dense = slice(GROUP * v, GROUP * (v + 1))

                own = side_of(tiles.at[slot], wide, pair, pair % 2, entry(table, n, 2 * pair + 1), v)
                joint = (own * (below, above, left)[pair // 2][pair % 2, 1, dense].astype(F32)).astype(BF16)
                far = (below, above, left)[pair // 2][pair % 2, 0, dense].astype(F32).astype(I32)
                return (buffers[slot, pair, dense], joint), (far, joint)

            strip_products(sums[pair % 2], strips)
            if pair > 0:
                finish(pair - 1)
        finish(OUTER_BATCH - 1)

    with_sums(steps)

    @pl.when(n == 0)
    def _():
        out_ref[:, : len(INNER) * 16] = inner[...]


def all_sums(px, w, below, above, left, inner):
    count = len(OUTER)
    vmem = pl.BlockSpec(memory_space=pltpu.VMEM)
    return pl.pallas_call(
        functools.partial(outer_kernel, OUTER.reshape(count // OUTER_BATCH, 2 * OUTER_BATCH)),
        grid=(count // OUTER_BATCH,),
        in_specs=[pl.BlockSpec(memory_space=pl.ANY)] * 2 + [vmem] * 4,
        out_specs=vmem,
        scratch_shapes=[
            pltpu.VMEM((2, OUTER_BATCH, CHUNKS, LANES), I32),
            pltpu.VMEM((2, OUTER_BATCH, LINES, LANES), BF16),
            pltpu.VMEM((2, LINES, LANES), F32),
            pltpu.SemaphoreType.DMA((2, OUTER_BATCH, 2)),
        ],
        out_shape=jax.ShapeDtypeStruct((2, (len(INNER) + count) * 16, 256), F32),
        compiler_params=pltpu.CompilerParams(vmem_limit_bytes=48 << 20),
        cost_estimate=pl.CostEstimate(
            flops=count * 4 * 256 * 256 * 8192, bytes_accessed=9 << 20, transcendentals=0
        ),
    )(px, w, below, above, left, inner)


def pieces(x):
    high = x.astype(BF16)
    rest = x - high.astype(F32)
    middle = rest.astype(BF16)
    return high, middle, (rest - middle.astype(F32)).astype(BF16)


def apply(coefficients, x):
    exact = coefficients.astype(BF16)
    return jnp.dot(
        jnp.concatenate([exact] * 3, 1), jnp.concatenate(pieces(x), 0), preferred_element_type=F32
    )


def apply_right(x, coefficients):
    exact = coefficients.astype(BF16)
    return jnp.dot(
        jnp.concatenate(pieces(x), 1), jnp.concatenate([exact] * 3, 0), preferred_element_type=F32
    )


def pair_results(first, second):
    iota = lambda shape, dim: lax.broadcasted_iota(I32, shape, dim)
    difference = first - second
    within = (iota((256, LANES), 0) // GROUP <= iota((256, LANES), 1)) & (iota((256, LANES), 1) < 16)
    row, other = iota((256, 256), 0), iota((256, 256), 1)
    before = (row // 16 == other // 16) & (other < row)
    earlier = jnp.sum(apply(before.astype(F32), difference), axis=1, keepdims=True)
    cumulative = apply_right(difference, within.astype(F32)) + earlier
    size = jnp.where(iota((256, LANES), 1) < 16, jnp.abs(cumulative), 0.0)
    pair, member = iota((32, 256), 0), iota((32, 256), 1)
    mine = pair % 16 == member // 16
    heights = jnp.where(mine, jnp.where(pair < 16, 1, member % 16 * 16), 0).astype(F32)
    sums = apply(heights, jnp.concatenate([first, second, size], 1))
    lower = (iota((16, 256), 1) // GROUP).astype(F32) + 0.5
    reduce = lambda x: jnp.sum(x, axis=1, keepdims=True)
    total = reduce(sums[:16, :256])
    mean_first = reduce(sums[:16, :256] * lower + sums[16:, :256]) / total
    mean_second = reduce(sums[:16, 256:512] * lower + sums[16:, 256:512]) / total
    distance = reduce(sums[:16, 512:]) / total
    mismatch = (distance - jnp.abs(mean_first - mean_second)) / mismatch_scale
    confidence = 1.0 / (0.25 + mismatch * mismatch)
    offset = jnp.log(mean_second) - jnp.log(mean_first)
    number, lane = iota((16, LANES), 0), iota((16, LANES), 1)
    spread = jnp.where(number == lane, confidence, jnp.where(number == lane - 16, offset, 0.0))
    return jnp.sum(jnp.where(total > 0, spread, 0.0), axis=0, keepdims=True)


def results_kernel(sums, out_ref):
    out_ref[...] = jnp.broadcast_to(pair_results(sums[0], sums[1]), out_ref.shape)


def results(sums, devices):
    return pl.pallas_call(
        results_kernel,
        in_specs=[pl.BlockSpec(memory_space=pltpu.VMEM)],
        out_specs=pl.BlockSpec(memory_space=pltpu.VMEM),
        out_shape=jax.ShapeDtypeStruct((devices, LANES), F32),
        compiler_params=pltpu.CompilerParams(vmem_limit_bytes=16 << 20),
    )(sums)


def on_grid(gathered, height, count_y):
    devices = gathered.shape[0]
    slot = lax.broadcasted_iota(I32, (LANES, LANES), 0)
    lane = lax.broadcasted_iota(I32, (LANES, LANES), 1)
    c, odd, right = lane % 4, lane // 32 % 2, lane // 64 == 1
    offset_slots = 16 * odd
    edge = right & (c == 3)
    slots = [
        jnp.where(edge, 14, jnp.where(right, 4 + c, c)),
        jnp.where(edge, 15, jnp.where(right, 7 + c, jnp.where(c < 2, 10 + c, -100))),
        jnp.where(right | (c < 2), -100, 10 + c),
    ]
    choose = jnp.concatenate([(slot == s + offset_slots).astype(F32) for s in slots], 1)
    chosen = apply_right(gathered, choose)
    device = lax.broadcasted_iota(I32, (devices, LANES), 0)
    lane = lax.broadcasted_iota(I32, (devices, LANES), 1)
    shifted = ((lane // 64 == 1) & (lane % 4 == 3)).astype(I32)
    here = device // count_y == lane % 32 // 4 + shifted
    parts = [jnp.where(here, chosen[:, LANES * k : LANES * (k + 1)], 0.0) for k in range(3)]
    row = lax.broadcasted_iota(I32, (height, devices), 0)
    top = lax.broadcasted_iota(I32, (height, devices), 1) % count_y * 2
    place = jnp.concatenate([(row == top + k).astype(F32) for k in (0, 1, -1)], 1)
    return apply(place, jnp.concatenate(parts, 0))


def sweep_kernel(height, width, count_y, where_ref, gathered, adjacency, out_ref, held, links, gain_ref, arrived):
    copy = pltpu.make_async_copy(adjacency, held, arrived)
    copy.start()
    grid = on_grid(gathered[...], height, count_y)
    links[...] = jnp.zeros_like(links)
    copy.wait()
    links[:, :, :width] = held[...]
    row = lax.broadcasted_iota(I32, (height, LANES), 0)
    column = lax.broadcasted_iota(I32, (height, LANES), 1)
    below = (links[1] > 0) & (row < height - 1) & (column < width)
    beside = (links[0] > 0) & (column < width - 1)

    def lanes_of(k, present):
        values = grid if k == 0 else pltpu.roll(grid, LANES - 32 * k, 1)
        return jnp.where(present, values, 0.0)

    conf_down, off_down = lanes_of(0, below), lanes_of(1, below)
    conf_right, off_right = lanes_of(2, beside), lanes_of(3, beside)
    up = lambda a: pltpu.roll(a, 1, 0)
    down = lambda a: pltpu.roll(a, height - 1, 0)
    lefts = lambda a: pltpu.roll(a, 1, 1)
    rights = lambda a: pltpu.roll(a, LANES - 1, 1)
    conf_up, off_up = up(conf_down), -up(off_down)
    conf_left, off_left = lefts(conf_right), -lefts(off_right)
    scale = 1.0 / (anchor_weight + conf_up + conf_down + conf_left + conf_right)
    constant = scale * (
        conf_up * off_up + conf_down * off_down + conf_left * off_left + conf_right * off_right
    )
    a_up, a_down, a_left, a_right = (scale * a for a in (conf_up, conf_down, conf_left, conf_right))

    ones = a_up + a_down + a_left + a_right
    columns = down(a_up) + up(a_down) + rights(a_left) + lefts(a_right)

    def mean(a):
        by_column = jnp.sum(a, axis=0, keepdims=True)
        return jnp.sum(by_column, axis=1, keepdims=True) * (1.0 / (height * width))

    mean_constant, mean_ones = mean(constant), mean(ones)

    def sweep(_, state):
        fresh, average = state
        spread = (
            (a_up * up(fresh) + a_down * down(fresh))
            + (a_left * lefts(fresh) + a_right * rights(fresh))
            + constant
        )
        later = mean(columns * fresh) + (mean_constant - average * mean_ones)
        return spread - average * ones, later

    fresh, average = lax.fori_loop(0, ITERS - 1, sweep, (constant, mean_constant), unroll=True)
    gain = fresh - average
    gain_ref[...] = pltpu.roll(gain, LANES - where_ref[1] * COLS, 1)
    out_ref[...] = gain_ref[pl.ds(where_ref[0] * ROWS, ROWS), :COLS]


def sweeps(gathered, adjacency, where):
    height, width = adjacency.shape[1:]
    return pl.pallas_call(
        functools.partial(sweep_kernel, height, width, height // ROWS),
        in_specs=[
            pl.BlockSpec(memory_space=pltpu.SMEM),
            pl.BlockSpec(memory_space=pltpu.VMEM),
            pl.BlockSpec(memory_space=pl.ANY),
        ],
        out_specs=pl.BlockSpec(memory_space=pltpu.VMEM),
        out_shape=jax.ShapeDtypeStruct((ROWS, COLS), F32),
        scratch_shapes=[
            pltpu.VMEM(adjacency.shape, I32),
            pltpu.VMEM((2, height, LANES), I32),
            pltpu.VMEM((height, LANES), F32),
            pltpu.SemaphoreType.DMA,
        ],
        compiler_params=pltpu.CompilerParams(vmem_limit_bytes=8 << 20),
    )(where, gathered, adjacency)


def body(pixels, weights, adjacency):
    px = pixels.reshape(ROWS * COLS, 4, CHUNKS, LANES).transpose(0, 2, 1, 3)
    w = weights.reshape(ROWS * COLS, 4, CHUNKS, LANES).transpose(0, 2, 1, 3)
    w = w.reshape(ROWS * COLS, LINES, LANES)
    count_x, count_y = lax.axis_size("gx"), lax.axis_size("gy")
    ahead = lambda n: [(i, i + 1) for i in range(n - 1)]
    back = lambda n: [(i + 1, i) for i in range(n - 1)]
    below, above, left = packed(px, w)
    below = lax.ppermute(below, "gy", back(count_y))
    above = lax.ppermute(above, "gy", ahead(count_y))
    left = lax.ppermute(left, "gx", ahead(count_x))
    inner = inner_sums(px, w)
    sums = all_sums(px, w, below, above, left, inner)
    gathered = lax.all_to_all(results(sums, count_x * count_y), ALL, 0, 0, tiled=True)
    where = jnp.stack([lax.axis_index("gy"), lax.axis_index("gx")]).astype(I32)
    return sweeps(gathered, adjacency, where)


def solution(mesh):
    return jax.shard_map(
        body,
        mesh=mesh,
        in_specs=(P("gy", "gx", None, None), P("gy", "gx", None, None), P()),
        out_specs=P("gy", "gx"),
        check_vma=False,
    )
```
